32 devices in a mesh: groups: 2 (over y), adapter: 4 (over z), tensor: 4 (over x, core).
Axes of the slice: x: 2, y: 2, z: 4, core: 2. Of those that a mesh axis runs over, the one named last changes fastest.
Arguments:
- tokens: bfloat16 [256, 8192], P(('groups', 'adapter')), parts along dimension 0, may hold values from -6 to 6
- attention_gain: float32 [8192], replicated, may hold values from 0.5 to 1.5
- query_weight: bfloat16 [8192, 4096], P('adapter', 'tensor'), may hold values from -0.0625 to 0.0625
- key_weight: bfloat16 [8192, 512], P('adapter', 'tensor'), may hold values from -0.0625 to 0.0625
- value_weight: bfloat16 [8192, 512], P('adapter', 'tensor'), may hold values from -0.0625 to 0.0625
- speaker_question_lowering: bfloat16 [8192, 32, 64], P('tensor', 'adapter'), may hold values from -0.0625 to 0.0625
- speaker_question_raising: bfloat16 [32, 64, 4096], P('adapter', None, 'tensor'), may hold values from -0.75 to 0.75
- speaker_content_lowering: bfloat16 [8192, 32, 64], P('tensor', 'adapter'), may hold values from -0.0625 to 0.0625
- speaker_content_raising: bfloat16 [32, 64, 512], P('adapter', None, 'tensor'), may hold values from -0.75 to 0.75
- rotated_key_cache: bfloat16 [256, 4, 128, 128], P(('groups', 'adapter'), 'tensor'), parts along dimension 0, may hold values from -400 to 400
- stored_value_cache: bfloat16 [256, 4, 128, 128], P(('groups', 'adapter'), 'tensor'), parts along dimension 0, may hold values from -6 to 6
- sequence_speaker_label: int32 [256], P(('groups', 'adapter')), parts along dimension 0, may hold values from 0 to 31, as said below
- lengths: int32 [256], P(('groups', 'adapter')), parts along dimension 0, may hold values from 1 to 127, as said below
- output_weight: bfloat16 [4096, 8192], P('tensor', 'adapter'), may hold values from -0.09375 to 0.09375
- closing_gain: float32 [8192], replicated, may hold values from 0.5 to 1.5
- codebook_weight: bfloat16 [8192, 16384], P('adapter', 'tensor'), may hold values from -0.19921875 to 0.19921875
- delays: int32 [8], replicated, may hold values from 0 to 63
Outputs:
- hidden: bfloat16 [256, 8192], P(('groups', 'tensor'), 'adapter'), parts along dimension 0
- logits: float32 [256, 8, 2048], P(('groups', 'adapter'), 'tensor'), parts along dimension 0
The draws below stay inside these ranges and needn't reach their ends.
There are 2 independent parts, one for each index of `groups`. The reference program is written for one: setup_inputs(seed, part) draws one part's arguments, and reference() takes and returns one part's arrays. A program takes and returns all parts, laid end to end along the dimension named above; an argument that names none is the same for every part. Nothing has to cross between parts.
Inputs may be any that keep to these rules, and one draw needn't show every extreme that they name: Call sequence_speaker_label[s] // 8 the owner of stream s. Among the 32 streams of one index of adapter, no owner is named more than 16 times; in every draw some owner is named 16 times within the streams of every index of adapter. `lengths`: some stream reaches the largest length.
All inputs are finite; a program needn't handle non-finite values.
Results may differ from the reference program's by a relative error of at most 0.0065.
The reference program's roundings to bfloat16 on the way count: a program that leaves them out, or rounds other values in their place, can miss the bound.
Values may be sent and summed in bfloat16 or wider, within the bound.
No kernel may reach another device: no remote copies, remote signals or barrier semaphores. Data moves between devices by JAX's collectives and lax.ppermute only.
A program may use at most 128 MiB of HBM per device.

```python
import jax
import jax.numpy as jnp
from jax import lax

MODEL_DIMENSION = 8192
HEAD_DIM = 128
HEADS = 32
KV_HEADS = 4
ADAPTER_RANK = 64
VOICE_DEV = 8
CB = 8
VOC = 2048
STR_DEV = 32
CTX = 128
QUERY_WIDTH = 4096
KEY_VALUE_WIDTH = 512
STREAMS = 128
VOICE_COUNT = 32
CAP = 16
N_ADAPTER = 4


def draw_sequence_speaker_label(key, part):
    key = jax.random.fold_in(key, 11)
    keys = jax.random.split(key, 5)
    picks = STR_DEV // CAP
    owner_range = jnp.arange(N_ADAPTER, dtype=jnp.int32)
    owner_bias = jax.random.randint(keys[0], (N_ADAPTER,), 0, 4) * 300
    hot_owner = jax.random.randint(keys[1], (), 0, N_ADAPTER)
    owner_bias = jnp.where(owner_range == hot_owner, 100000, owner_bias)
    noise_part = jax.random.randint(keys[2], (N_ADAPTER, N_ADAPTER), 0, 1000)
    owner_score = (owner_bias[None, :] + noise_part) * N_ADAPTER + owner_range[None, :]
    chosen = lax.top_k(owner_score, picks + 1)[1].astype(jnp.int32)
    owners = jnp.repeat(chosen[:, :picks], CAP, axis=1)
    owners = owners.at[:, STR_DEV - 1].set(chosen[:, picks])
    order_score = jax.random.randint(keys[3], (N_ADAPTER, STR_DEV), 0, 1 << 20) * STR_DEV + jnp.arange(STR_DEV, dtype=jnp.int32)[None, :]
    ordering = jnp.argsort(order_score, axis=1)
    owners = jnp.take_along_axis(owners, ordering, axis=1)
    local_voice = jax.random.randint(keys[4], (N_ADAPTER, STR_DEV), 0, VOICE_DEV)
    return (owners * VOICE_DEV + local_voice).reshape(-1).astype(jnp.int32)


def draw_lengths(key, part):
    key = jax.random.fold_in(key, 12)
    keys = jax.random.split(key, 3)
    first_draw = jax.random.randint(keys[0], (STREAMS,), 1, CTX)
    second_draw = jax.random.randint(keys[1], (STREAMS,), 1, CTX)
    longest_spot = jax.random.randint(keys[2], (), 0, STREAMS)
    chosen_len = jnp.minimum(first_draw, second_draw)
    return jnp.where(jnp.arange(STREAMS) == longest_spot, CTX - 1, chosen_len).astype(jnp.int32)


def draw_rotated_key_cache(key, part):
    key = jax.random.fold_in(key, 13)
    keys = jax.random.split(key, 1)
    base_vals = jax.random.normal(keys[0], (STREAMS, KV_HEADS, CTX, HEAD_DIM), jnp.float32)
    values = jnp.clip(base_vals, -6.0, 6.0)
    return values.astype(jnp.bfloat16)


def place_ends(values, key, smallest, high):
    longest = values.shape.index(max(values.shape))
    spots = []
    for shift in (0, 1):
        where = [jax.random.randint(jax.random.fold_in(key, axis), (), 0, length) for axis, length in enumerate(values.shape)]
        where[longest] = (where[longest] + shift) % values.shape[longest]
        spots.append(tuple(where))
    return values.at[spots[0]].set(smallest).at[spots[1]].set(high)


def steps_of(rng, dims, pieces, smallest, largest):
    loudness = 1.0
    for position, shards_of in pieces:
        heights = jax.random.uniform(jax.random.fold_in(jax.random.fold_in(rng, 6), position), (shards_of,), jnp.float32, smallest / len(pieces), largest / len(pieces))
        loudness = loudness * jnp.repeat(jnp.exp(heights), dims[position] // shards_of).reshape((-1,) + (1,) * (len(dims) - 1 - position))
    return loudness


def bell_draw(stream_key, dims, width, limit, cuts=(), kind=jnp.bfloat16):
    array = width * jax.random.normal(stream_key, dims, jnp.float32)
    if cuts:
        array = array * steps_of(stream_key, dims, cuts, -0.22, 0.18)
    return jnp.clip(array, -limit, limit).astype(kind)


def setup_inputs(seed: int = 0, part: int = 0) -> dict:
    seeds = jax.random.split(jax.random.key(seed), 18)
    own_keys = jax.random.split(jax.random.fold_in(seeds[17], part), 18)
    tokens = bell_draw(own_keys[0], (STREAMS, MODEL_DIMENSION), 1.0, 6.0, ((0, 4),))
    attention_gain = jnp.clip(1.0 + 0.1 * jax.random.normal(seeds[1], (MODEL_DIMENSION,), jnp.float32), 0.5, 1.5)
    query_weight = bell_draw(seeds[2], (MODEL_DIMENSION, QUERY_WIDTH), MODEL_DIMENSION ** -0.5, 0.0625, ((0, 4), (1, 4)))
    key_weight = bell_draw(seeds[3], (MODEL_DIMENSION, KEY_VALUE_WIDTH), MODEL_DIMENSION ** -0.5, 0.0625, ((0, 4), (1, 4)))
    value_weight = bell_draw(seeds[4], (MODEL_DIMENSION, KEY_VALUE_WIDTH), MODEL_DIMENSION ** -0.5, 0.0625, ((0, 4), (1, 4)))
    speaker_question_lowering = bell_draw(seeds[5], (MODEL_DIMENSION, VOICE_COUNT, ADAPTER_RANK), MODEL_DIMENSION ** -0.5, 0.0625, ((0, 4), (1, 4)))
    speaker_question_raising = bell_draw(seeds[6], (VOICE_COUNT, ADAPTER_RANK, QUERY_WIDTH), ADAPTER_RANK ** -0.5, 0.75, ((0, 4), (2, 4)))
    speaker_content_lowering = bell_draw(seeds[7], (MODEL_DIMENSION, VOICE_COUNT, ADAPTER_RANK), MODEL_DIMENSION ** -0.5, 0.0625, ((0, 4), (1, 4)))
    speaker_content_raising = bell_draw(seeds[8], (VOICE_COUNT, ADAPTER_RANK, KEY_VALUE_WIDTH), ADAPTER_RANK ** -0.5, 0.75, ((0, 4), (2, 4)))
    rotated_key_cache = draw_rotated_key_cache(jax.random.fold_in(jax.random.fold_in(seeds[17], part), 71), part)
    stored_value_cache = bell_draw(own_keys[10], (STREAMS, KV_HEADS, CTX, HEAD_DIM), 1.0, 6.0, ((0, 4), (1, 4)))
    sequence_speaker_label = draw_sequence_speaker_label(jax.random.fold_in(jax.random.fold_in(seeds[17], part), 71), part)
    lengths = draw_lengths(jax.random.fold_in(jax.random.fold_in(seeds[17], part), 71), part)
    output_weight = bell_draw(seeds[13], (QUERY_WIDTH, MODEL_DIMENSION), QUERY_WIDTH ** -0.5, 0.09375, ((0, 4), (1, 4)))
    closing_gain = jnp.clip(1.0 + 0.1 * jax.random.normal(seeds[14], (MODEL_DIMENSION,), jnp.float32), 0.5, 1.5)
    codebook_weight = bell_draw(seeds[15], (MODEL_DIMENSION, CB * VOC), 0.033, 0.19921875, ((0, 4), (1, 4)))
    delays = place_ends(jax.random.randint(seeds[16], (CB,), 0, CTX // 2), jax.random.fold_in(seeds[16], 1), 0, (CTX // 2) - 1).astype(jnp.int32)
    return dict(tokens=tokens, attention_gain=attention_gain, query_weight=query_weight, key_weight=key_weight, value_weight=value_weight, speaker_question_lowering=speaker_question_lowering, speaker_question_raising=speaker_question_raising, speaker_content_lowering=speaker_content_lowering, speaker_content_raising=speaker_content_raising, rotated_key_cache=rotated_key_cache, stored_value_cache=stored_value_cache, sequence_speaker_label=sequence_speaker_label, lengths=lengths, output_weight=output_weight, closing_gain=closing_gain, codebook_weight=codebook_weight, delays=delays)


ROPE_BASE = 500000.0
NORM_EPS = 1e-05
ADAPTER_SCALE = 0.5

def rms_norm(values, gain):
    mean_square = lax.optimization_barrier(jnp.mean(values * values, axis=-1, keepdims=True))
    return (values * lax.rsqrt(mean_square + NORM_EPS) * gain).astype(jnp.bfloat16)

def rotate(values, positions):
    head_dim = values.shape[-1]
    half_dim = head_dim // 2
    spacing = jnp.arange(half_dim, dtype=jnp.float32) * (2.0 / head_dim)
    angles = positions.astype(jnp.float32)[:, None] * jnp.power(ROPE_BASE, -spacing)[None, :]
    new_shape = (values.shape[0],) + (1,) * (values.ndim - 2) + (half_dim,)
    cosine = jnp.cos(angles).reshape(new_shape)
    sine = jnp.sin(angles).reshape(new_shape)
    first_half = values[..., :half_dim]
    second_half = values[..., half_dim:]
    return jnp.concatenate([first_half * cosine - second_half * sine, first_half * sine + second_half * cosine], axis=-1)

def correction_terms(rescaled_hidden_state, sequence_speaker_label, lowering_projection, raising_projection):

    def block(inputs):
        rows_block, ids_block = inputs
        down_sel = jnp.take(lowering_projection, ids_block, axis=1).astype(jnp.float32)
        value_down_result = jnp.einsum('sd,dsr->sr', rows_block.astype(jnp.float32), down_sel).astype(jnp.bfloat16)
        selected_up_matrix = jnp.take(raising_projection, ids_block, axis=0).astype(jnp.float32)
        value_up_output = jnp.einsum('wa,waq->wq', value_down_result.astype(jnp.float32), selected_up_matrix) * ADAPTER_SCALE
        return value_up_output.astype(jnp.bfloat16)
    rows_all = rescaled_hidden_state.reshape(N_ADAPTER, STR_DEV, MODEL_DIMENSION)
    ids_all = sequence_speaker_label.reshape(N_ADAPTER, STR_DEV)
    result = lax.map(block, (rows_all, ids_all))
    return result.reshape(STREAMS, -1)

def reference(tokens, attention_gain, query_weight, key_weight, value_weight, speaker_question_lowering, speaker_question_raising, speaker_content_lowering, speaker_content_raising, rotated_key_cache, stored_value_cache, sequence_speaker_label, lengths, output_weight, closing_gain, codebook_weight, delays):
    tok_f = tokens.astype(jnp.float32)
    rescaled_hidden_state = rms_norm(tok_f, attention_gain)
    plain_query = jnp.dot(rescaled_hidden_state, query_weight, preferred_element_type=jnp.float32)
    key_base = jnp.dot(rescaled_hidden_state, key_weight, preferred_element_type=jnp.float32)
    plain_value = jnp.dot(rescaled_hidden_state, value_weight, preferred_element_type=jnp.float32)
    question_raised_product = correction_terms(rescaled_hidden_state, sequence_speaker_label, speaker_question_lowering, speaker_question_raising)
    content_raised_product = correction_terms(rescaled_hidden_state, sequence_speaker_label, speaker_content_lowering, speaker_content_raising)
    group_size = HEADS // KV_HEADS
    adapted_query = (plain_query + question_raised_product.astype(jnp.float32)).reshape(STREAMS, KV_HEADS, group_size, HEAD_DIM)
    query = rotate(adapted_query, lengths).astype(jnp.bfloat16)
    key_new = rotate(key_base.reshape(STREAMS, KV_HEADS, HEAD_DIM), lengths).astype(jnp.bfloat16)
    value_new = (plain_value + content_raised_product.astype(jnp.float32)).reshape(STREAMS, KV_HEADS, HEAD_DIM).astype(jnp.bfloat16)
    scale_factor = 1.0 / HEAD_DIM ** 0.5
    query_f = query.astype(jnp.float32)
    scores = jnp.einsum('skgd,skcd->skgc', query_f, rotated_key_cache.astype(jnp.float32)) * scale_factor
    own_score = jnp.einsum('skgd,skd->skg', query_f, key_new.astype(jnp.float32)) * scale_factor
    valid = (jnp.arange(CTX)[None, :] < lengths[:, None])[:, None, None, :]
    masked = jnp.where(valid, scores, -1e+30)
    top_score = jnp.maximum(lax.optimization_barrier(jnp.max(masked, axis=-1)), own_score)
    weights_all = jnp.where(valid, jnp.exp(scores - top_score[..., None]), 0.0)
    own_weight = jnp.exp(own_score - top_score)
    total = lax.optimization_barrier(jnp.sum(weights_all, axis=-1)) + own_weight
    probs = (weights_all / total[..., None]).astype(jnp.bfloat16)
    own_prob = (own_weight / total).astype(jnp.bfloat16)
    mixed = jnp.einsum('skgc,skcd->skgd', probs.astype(jnp.float32), stored_value_cache.astype(jnp.float32))
    mixed = mixed + own_prob.astype(jnp.float32)[..., None] * value_new.astype(jnp.float32)[:, :, None, :]
    attended = mixed.astype(jnp.bfloat16).reshape(STREAMS, QUERY_WIDTH)
    hidden = (tok_f + jnp.dot(attended, output_weight, preferred_element_type=jnp.float32)).astype(jnp.bfloat16)
    final_normed = rms_norm(hidden.astype(jnp.float32), closing_gain)
    logit_flat = jnp.dot(final_normed, codebook_weight, preferred_element_type=jnp.float32)
    active = (lengths[:, None] >= delays[None, :]).astype(jnp.float32)
    logits = logit_flat.reshape(STREAMS, CB, VOC) * active[:, :, None]
    return (hidden, logits)
```

```python
import jax
import jax.numpy as jnp
from jax import lax
from jax.sharding import PartitionSpec as P

CB = 8
VOC = 2048


ROPE_BASE = 500000.0
NORM_EPS = 1e-05
ADAPTER_SCALE = 0.5
LOGIT_PARTS = 4


def rotate(values, positions):
    head_dim = values.shape[-1]
    half_dim = head_dim // 2
    spacing = jnp.arange(half_dim, dtype=jnp.float32) * (2.0 / head_dim)
    angles = positions.astype(jnp.float32)[:, None] * jnp.power(ROPE_BASE, -spacing)[None, :]
    new_shape = (values.shape[0],) + (1,) * (values.ndim - 2) + (half_dim,)
    cosine = jnp.cos(angles).reshape(new_shape)
    sine = jnp.sin(angles).reshape(new_shape)
    first_half = values[..., :half_dim]
    second_half = values[..., half_dim:]
    return jnp.concatenate(
        [first_half * cosine - second_half * sine, first_half * sine + second_half * cosine],
        axis=-1,
    )


def swap(value, axis, distance):
    size = lax.axis_size(axis)
    return lax.ppermute(value, axis, [(i, i ^ distance) for i in range(size)])


def take_block(array, index, size, axis=0):
    return lax.dynamic_slice_in_dim(array, index * size, size, axis)


def per_device_four(
    tokens,
    attention_gain,
    query_weight,
    key_weight,
    value_weight,
    speaker_question_lowering,
    speaker_question_raising,
    speaker_content_lowering,
    speaker_content_raising,
    rotated_key_cache,
    stored_value_cache,
    sequence_speaker_label,
    lengths,
    output_weight,
    closing_gain,
    codebook_weight,
    delays,
):
    n_adapter = lax.axis_size("adapter")
    peers = range(1, n_adapter)
    a = lax.axis_index("adapter")
    t = lax.axis_index("tensor")
    core = t % 2
    str_dev, model_width = tokens.shape
    half = str_dev // 2
    d_slice = model_width // n_adapter
    voices, rank = speaker_question_raising.shape[:2]
    query_columns = query_weight.shape[1]
    key_value_columns = key_weight.shape[1]

    tok_f = tokens.astype(jnp.float32)
    inverse = lax.rsqrt(jnp.mean(tok_f * tok_f, axis=-1, keepdims=True) + NORM_EPS)
    normed = (tok_f * inverse * attention_gain).astype(jnp.bfloat16)

    my_half = take_block(normed, core, half)
    came = [swap(take_block(my_half, a ^ k, d_slice, 1), "adapter", k) for k in peers]

    slot_cap = max(2, 2 * str_dev // n_adapter)
    owner_ids = sequence_speaker_label // voices
    local_voice = sequence_speaker_label % voices
    same_owner = owner_ids[:, None] == owner_ids[None, :]
    earlier = jnp.arange(str_dev)[:, None] > jnp.arange(str_dev)[None, :]
    owner_rank = jnp.sum((same_owner & earlier).astype(jnp.int32), axis=1)
    slot_ids = (owner_ids ^ a) * slot_cap + owner_rank
    placing = (slot_ids[None, :] == jnp.arange(n_adapter * slot_cap)[:, None]).astype(jnp.bfloat16)
    voice_onehot = (local_voice[:, None] == jnp.arange(128)[None, :]).astype(jnp.bfloat16)
    sent_rows = jnp.dot(
        placing,
        jnp.concatenate([take_block(normed, t, d_slice, 1), voice_onehot], axis=1),
        preferred_element_type=jnp.float32,
    ).astype(jnp.bfloat16)
    rows_in = [sent_rows[:slot_cap]] + [
        swap(sent_rows[k * slot_cap : (k + 1) * slot_cap], "adapter", k) for k in peers
    ]

    came = jnp.stack(came)
    other = swap(came, "tensor", 1)
    first = jnp.where(core == 0, came, other)
    second = jnp.where(core == 0, other, came)
    arrived = jnp.concatenate([first, second], axis=1).reshape(-1, d_slice)
    norm_cols = jnp.concatenate([take_block(normed, a, d_slice, 1), arrived], axis=0)
    base = jnp.concatenate(
        [
            jnp.dot(norm_cols, weight, preferred_element_type=jnp.float32)
            for weight in (query_weight, key_weight, value_weight)
        ],
        axis=1,
    )
    projected = base[:str_dev]
    for k in peers:
        projected = projected + swap(base[k * str_dev : (k + 1) * str_dev], "adapter", k)

    rows = jnp.concatenate(rows_in, axis=0)
    onehot_b = rows[:, d_slice : d_slice + voices]
    onehot_f = onehot_b.astype(jnp.float32)
    flat_rows = rows[:, :d_slice]
    downs = []
    for lowering in (speaker_question_lowering, speaker_content_lowering):
        every = jnp.dot(
            flat_rows, lowering.reshape(d_slice, voices * rank), preferred_element_type=jnp.float32
        )
        downs.append(jnp.sum(onehot_f[:, :, None] * every.reshape(-1, voices, rank), axis=1))
    down = jnp.concatenate(downs, axis=1)
    down = down + swap(down, "tensor", 1)
    down = (down + swap(down, "tensor", 2)).astype(jnp.bfloat16)
    ups = []
    for i, raising in enumerate((speaker_question_raising, speaker_content_raising)):
        spread = (
            onehot_b[:, :, None] * down[:, None, i * rank : (i + 1) * rank]
        ).reshape(-1, voices * rank)
        up = jnp.dot(
            spread, raising.reshape(voices * rank, -1), preferred_element_type=jnp.float32
        )
        ups.append((up * ADAPTER_SCALE).astype(jnp.bfloat16))
    outgoing = jnp.concatenate(ups, axis=1)
    returned = jnp.concatenate(
        [outgoing[:slot_cap]]
        + [swap(outgoing[k * slot_cap : (k + 1) * slot_cap], "adapter", k) for k in peers],
        axis=0,
    )
    adapter_summands = jnp.einsum(
        "ms,mc->sc", placing, returned, preferred_element_type=jnp.float32
    )

    kv_local, ctx_len, head_dim = rotated_key_cache.shape[1:]
    group_size = query_columns // (kv_local * head_dim)
    query = rotate(
        (projected[:, :query_columns] + adapter_summands[:, :query_columns]).reshape(
            str_dev, kv_local, group_size, head_dim
        ),
        lengths,
    ).astype(jnp.bfloat16)
    key_base = projected[:, query_columns : query_columns + key_value_columns]
    key_new = rotate(key_base.reshape(str_dev, kv_local, head_dim), lengths).astype(jnp.bfloat16)
    value_new = (
        (projected[:, query_columns + key_value_columns :] + adapter_summands[:, query_columns:])
        .reshape(str_dev, kv_local, head_dim)
        .astype(jnp.bfloat16)
    )
    scale_factor = 1.0 / head_dim**0.5
    scores = (
        jnp.einsum("skgd,skcd->skgc", query, rotated_key_cache, preferred_element_type=jnp.float32)
        * scale_factor
    )
    own_score = (
        jnp.einsum("skgd,skd->skg", query, key_new, preferred_element_type=jnp.float32)
        * scale_factor
    )
    valid = (jnp.arange(ctx_len)[None, :] < lengths[:, None])[:, None, None, :]
    masked = jnp.where(valid, scores, -1e30)
    top_score = jnp.maximum(jnp.max(masked, axis=-1), own_score)
    weights_all = jnp.where(valid, jnp.exp(scores - top_score[..., None]), 0.0)
    own_weight = jnp.exp(own_score - top_score)
    total = jnp.sum(weights_all, axis=-1) + own_weight
    probs = (weights_all / total[..., None]).astype(jnp.bfloat16)
    own_prob = (own_weight / total).astype(jnp.bfloat16)
    mixed = jnp.einsum(
        "skgc,skcd->skgd", probs, stored_value_cache, preferred_element_type=jnp.float32
    )
    mixed = (
        mixed
        + own_prob.astype(jnp.float32)[..., None] * value_new.astype(jnp.float32)[:, :, None, :]
    )
    attended = mixed.astype(jnp.bfloat16).reshape(str_dev, query_columns)

    raw = lax.ppermute(
        take_block(tokens, t, d_slice, 1),
        ("adapter", "tensor"),
        [(i * n_adapter + j, j * n_adapter + i) for i in range(n_adapter) for j in range(n_adapter)],
    )
    gathered = jnp.concatenate(
        [attended] + [swap(attended, "adapter", k) for k in peers], axis=0
    )
    partial_out = jnp.dot(gathered, output_weight, preferred_element_type=jnp.float32)
    turn = a ^ t
    near = swap(
        jnp.concatenate(
            [take_block(partial_out, turn ^ 1, str_dev), take_block(partial_out, turn ^ 3, str_dev)]
        ),
        "tensor",
        1,
    )
    far = take_block(partial_out, turn ^ 2, str_dev) + near[str_dev:]
    summed_out = take_block(partial_out, turn, str_dev) + near[:str_dev] + swap(far, "tensor", 2)
    hidden_out = (raw.astype(jnp.float32) + summed_out).astype(jnp.bfloat16)

    hidden_f = hidden_out.astype(jnp.float32)
    square = jnp.sum(hidden_f * hidden_f, axis=-1)
    square_pair = jnp.stack([square, swap(square, "tensor", 2)])
    squares = jnp.concatenate([square_pair, swap(square_pair, "tensor", 1)]).reshape(-1)
    square_sum = squares
    for k in peers:
        square_sum = square_sum + swap(squares, "adapter", k)
    hidden_pair = jnp.concatenate([hidden_out, swap(hidden_out, "tensor", 2)])
    hidden_all = jnp.concatenate([hidden_pair, swap(hidden_pair, "tensor", 1)])
    final_slice = take_block(closing_gain, a, d_slice)
    final_normed = (
        hidden_all.astype(jnp.float32)
        * lax.rsqrt(square_sum / model_width + NORM_EPS)[:, None]
        * final_slice
    ).astype(jnp.bfloat16)

    books_local = CB // lax.axis_size("tensor")
    book_delays = take_block(delays, t, books_local)
    active = (lengths[:, None] >= book_delays[None, :]).astype(jnp.float32)
    place = jnp.array([0, 2, 1, 3], jnp.int32)
    parts = LOGIT_PARTS
    width = codebook_weight.shape[1] // parts
    outs = []
    for p in range(parts):
        partial = jnp.dot(
            final_normed,
            codebook_weight[:, p * width : (p + 1) * width],
            preferred_element_type=jnp.float32,
        )
        total_p = take_block(partial, place[turn], str_dev)
        for k in peers:
            block = take_block(partial, place[turn ^ k], str_dev)
            total_p = total_p + swap(
                (block * 32.0).astype(jnp.float16), "adapter", k
            ).astype(jnp.float32) * (1.0 / 32.0)
        outs.append(total_p)
    logits = jnp.concatenate(outs, axis=1).reshape(str_dev, books_local, VOC) * active[:, :, None]
    return (hidden_out, logits)


def per_device(
    tokens,
    attention_gain,
    query_weight,
    key_weight,
    value_weight,
    speaker_question_lowering,
    speaker_question_raising,
    speaker_content_lowering,
    speaker_content_raising,
    rotated_key_cache,
    stored_value_cache,
    sequence_speaker_label,
    lengths,
    output_weight,
    closing_gain,
    codebook_weight,
    delays,
):
    n_adapter = lax.axis_size("adapter")
    n_tensor = lax.axis_size("tensor")
    adapter_pos = lax.axis_index("adapter")
    tensor_pos = lax.axis_index("tensor")
    str_dev, model_width = tokens.shape
    all_streams = str_dev * n_adapter
    d_slice = model_width // n_adapter
    tensor_width = model_width // n_tensor
    tok_f = tokens.astype(jnp.float32)
    inverse = lax.rsqrt(jnp.mean(tok_f * tok_f, axis=-1, keepdims=True) + NORM_EPS)
    rescaled_hidden_state = (tok_f * inverse * attention_gain).astype(jnp.bfloat16)
    raw_cols, norm_cols = (
        lax.all_to_all(tokens, "adapter", split_axis=1, concat_axis=0, tiled=True),
        lax.all_to_all(rescaled_hidden_state, "adapter", split_axis=1, concat_axis=0, tiled=True),
    )
    query_columns = query_weight.shape[1]
    key_value_columns = key_weight.shape[1]
    weights_cat = jnp.concatenate([query_weight, key_weight, value_weight], axis=1)
    full_proj = jnp.dot(norm_cols, weights_cat, preferred_element_type=jnp.float32)
    summed = lax.psum(full_proj, "adapter")
    projected = lax.dynamic_slice_in_dim(summed, adapter_pos * str_dev, str_dev, 0)
    plain_query = projected[:, :query_columns]
    key_base = projected[:, query_columns : query_columns + key_value_columns]
    plain_value = projected[:, query_columns + key_value_columns :]
    voices_per_shard = speaker_question_raising.shape[0]
    adapter_rank_size = speaker_question_raising.shape[1]
    slot_cap = max(2, 2 * str_dev // n_adapter)
    slot_total = n_adapter * slot_cap
    owner_ids = sequence_speaker_label // voices_per_shard
    local_voice = sequence_speaker_label % voices_per_shard
    same_owner = owner_ids[:, None] == owner_ids[None, :]
    earlier = jnp.arange(str_dev)[:, None] > jnp.arange(str_dev)[None, :]
    owner_rank = jnp.sum((same_owner & earlier).astype(jnp.int32), axis=1)
    slot_ids = owner_ids * slot_cap + owner_rank
    placing = (slot_ids[None, :] == jnp.arange(slot_total)[:, None]).astype(jnp.bfloat16)
    voice_onehot = (local_voice[:, None] == jnp.arange(voices_per_shard)[None, :]).astype(
        jnp.bfloat16
    )
    normed_part = lax.dynamic_slice_in_dim(
        rescaled_hidden_state, tensor_pos * tensor_width, tensor_width, 1
    )
    send_rows = jnp.dot(placing, normed_part, preferred_element_type=jnp.float32).astype(
        jnp.bfloat16
    )
    send_voice = jnp.dot(placing, voice_onehot, preferred_element_type=jnp.float32).astype(
        jnp.bfloat16
    )
    send_rows = send_rows.reshape(n_adapter, slot_cap, tensor_width)
    send_voice = send_voice.reshape(n_adapter, slot_cap, voices_per_shard)
    query_down_matrix = speaker_question_lowering.reshape(
        tensor_width, voices_per_shard * adapter_rank_size
    )
    value_down_matrix = speaker_content_lowering.reshape(
        tensor_width, voices_per_shard * adapter_rank_size
    )
    query_up_matrix = speaker_question_raising.reshape(
        voices_per_shard * adapter_rank_size, query_columns
    )
    value_up_matrix = speaker_content_raising.reshape(
        voices_per_shard * adapter_rank_size, key_value_columns
    )
    rows_in = lax.all_to_all(send_rows, "adapter", split_axis=0, concat_axis=0, tiled=True)
    voices_in = lax.all_to_all(send_voice, "adapter", split_axis=0, concat_axis=0, tiled=True)
    item_count = rows_in.shape[1]
    flat_rows = rows_in.reshape(-1, tensor_width)
    onehot_b = voices_in.reshape(-1, voices_per_shard)
    onehot_f = onehot_b.astype(jnp.float32)
    all_q = jnp.dot(flat_rows, query_down_matrix, preferred_element_type=jnp.float32).reshape(
        -1, voices_per_shard, adapter_rank_size
    )
    all_v = jnp.dot(flat_rows, value_down_matrix, preferred_element_type=jnp.float32).reshape(
        -1, voices_per_shard, adapter_rank_size
    )
    down_q = jnp.sum(onehot_f[:, :, None] * all_q, axis=1)
    down_v = jnp.sum(onehot_f[:, :, None] * all_v, axis=1)
    down_q, down_v = lax.psum((down_q, down_v), "tensor")
    query_broadcast = (onehot_b[:, :, None] * down_q.astype(jnp.bfloat16)[:, None, :]).reshape(
        -1, voices_per_shard * adapter_rank_size
    )
    value_broadcast = (onehot_b[:, :, None] * down_v.astype(jnp.bfloat16)[:, None, :]).reshape(
        -1, voices_per_shard * adapter_rank_size
    )
    question_raised_product = (
        jnp.dot(query_broadcast, query_up_matrix, preferred_element_type=jnp.float32)
        * ADAPTER_SCALE
    ).astype(jnp.bfloat16)
    content_raised_product = (
        jnp.dot(value_broadcast, value_up_matrix, preferred_element_type=jnp.float32)
        * ADAPTER_SCALE
    ).astype(jnp.bfloat16)
    outgoing = jnp.concatenate([question_raised_product, content_raised_product], axis=1).reshape(
        n_adapter, item_count, query_columns + key_value_columns
    )
    returned = lax.all_to_all(outgoing, "adapter", split_axis=0, concat_axis=0, tiled=True)
    adapter_summands = jnp.einsum(
        "ms,mc->sc",
        placing,
        returned.reshape(slot_total, query_columns + key_value_columns),
        preferred_element_type=jnp.float32,
    )
    kv_local = rotated_key_cache.shape[1]
    head_dim = rotated_key_cache.shape[3]
    ctx_len = rotated_key_cache.shape[2]
    group_size = query_columns // (kv_local * head_dim)
    adapted_query = (plain_query + adapter_summands[:, :query_columns]).reshape(
        str_dev, kv_local, group_size, head_dim
    )
    query = rotate(adapted_query, lengths).astype(jnp.bfloat16)
    key_new = rotate(key_base.reshape(str_dev, kv_local, head_dim), lengths).astype(jnp.bfloat16)
    value_new = (
        (plain_value + adapter_summands[:, query_columns:])
        .reshape(str_dev, kv_local, head_dim)
        .astype(jnp.bfloat16)
    )
    scale_factor = 1.0 / head_dim**0.5
    scores = (
        jnp.einsum("skgd,skcd->skgc", query, rotated_key_cache, preferred_element_type=jnp.float32)
        * scale_factor
    )
    own_score = (
        jnp.einsum("skgd,skd->skg", query, key_new, preferred_element_type=jnp.float32)
        * scale_factor
    )
    valid = (jnp.arange(ctx_len)[None, :] < lengths[:, None])[:, None, None, :]
    masked = jnp.where(valid, scores, -1e30)
    top_score = jnp.maximum(jnp.max(masked, axis=-1), own_score)
    weights_all = jnp.where(valid, jnp.exp(scores - top_score[..., None]), 0.0)
    own_weight = jnp.exp(own_score - top_score)
    total = jnp.sum(weights_all, axis=-1) + own_weight
    probs = (weights_all / total[..., None]).astype(jnp.bfloat16)
    own_prob = (own_weight / total).astype(jnp.bfloat16)
    mixed = jnp.einsum(
        "skgc,skcd->skgd", probs, stored_value_cache, preferred_element_type=jnp.float32
    )
    mixed = (
        mixed
        + own_prob.astype(jnp.float32)[..., None] * value_new.astype(jnp.float32)[:, :, None, :]
    )
    attended = mixed.astype(jnp.bfloat16).reshape(str_dev, query_columns)
    partial_out = jnp.dot(
        lax.all_gather(attended, "adapter", axis=0, tiled=True),
        output_weight,
        preferred_element_type=jnp.float32,
    )
    final_slice = lax.dynamic_slice_in_dim(closing_gain, adapter_pos * d_slice, d_slice)
    rows_tensor = all_streams // n_tensor
    summed_out = lax.psum(partial_out, "tensor")
    hidden_all = (raw_cols.astype(jnp.float32) + summed_out).astype(jnp.bfloat16)
    hidden_f = hidden_all.astype(jnp.float32)
    square_sum = lax.psum(jnp.sum(hidden_f * hidden_f, axis=-1), "adapter")
    final_normed = (
        hidden_f * lax.rsqrt(square_sum / model_width + NORM_EPS)[:, None] * final_slice
    ).astype(jnp.bfloat16)
    hidden_out = lax.dynamic_slice_in_dim(hidden_all, tensor_pos * rows_tensor, rows_tensor, 0)
    logit_rows = lax.psum_scatter(
        jnp.dot(final_normed, codebook_weight, preferred_element_type=jnp.float32),
        "adapter",
        scatter_dimension=0,
        tiled=True,
    )
    books_local = CB // n_tensor
    book_delays = lax.dynamic_slice_in_dim(delays, tensor_pos * books_local, books_local)
    active = (lengths[:, None] >= book_delays[None, :]).astype(jnp.float32)
    logits = logit_rows.reshape(str_dev, books_local, VOC) * active[:, :, None]
    return (hidden_out, logits)


def solution(mesh):
    in_specs = (
        P(("groups", "adapter"), None),
        P(),
        P("adapter", "tensor"),
        P("adapter", "tensor"),
        P("adapter", "tensor"),
        P("tensor", "adapter", None),
        P("adapter", None, "tensor"),
        P("tensor", "adapter", None),
        P("adapter", None, "tensor"),
        P(("groups", "adapter"), "tensor", None, None),
        P(("groups", "adapter"), "tensor", None, None),
        P(("groups", "adapter")),
        P(("groups", "adapter")),
        P("tensor", "adapter"),
        P(),
        P("adapter", "tensor"),
        P(),
    )
    out_specs = (P(("groups", "tensor"), "adapter"), P(("groups", "adapter"), "tensor", None))
    four = mesh.shape["adapter"] == 4 and mesh.shape["tensor"] == 4
    return jax.shard_map(
        per_device_four if four else per_device, mesh=mesh, in_specs=in_specs, out_specs=out_specs, check_vma=False
    )
```

```python
import functools

import jax
import jax.numpy as jnp
from jax import lax
from jax.experimental import pallas as pl
from jax.experimental.pallas import tpu as pltpu
from jax.sharding import PartitionSpec as P

CB = 8
VOC = 2048


ROPE_BASE = 500000.0
NORM_EPS = 1e-05
ADAPTER_SCALE = 0.5
LOGIT_PARTS = 2


def rotate(values, positions):
    head_dim = values.shape[-1]
    half_dim = head_dim // 2
    spacing = jnp.arange(half_dim, dtype=jnp.float32) * (2.0 / head_dim)
    angles = positions.astype(jnp.float32)[:, None] * jnp.power(ROPE_BASE, -spacing)[None, :]
    new_shape = (values.shape[0],) + (1,) * (values.ndim - 2) + (half_dim,)
    cosine = jnp.cos(angles).reshape(new_shape)
    sine = jnp.sin(angles).reshape(new_shape)
    first_half = values[..., :half_dim]
    second_half = values[..., half_dim:]
    return jnp.concatenate(
        [first_half * cosine - second_half * sine, first_half * sine + second_half * cosine],
        axis=-1,
    )


def swap(value, axis, distance):
    size = lax.axis_size(axis)
    return lax.ppermute(value, axis, [(i, i ^ distance) for i in range(size)])


def take_block(array, index, size, axis=0):
    return lax.dynamic_slice_in_dim(array, index * size, size, axis)


def lowering_kernel(voices, rank, own_ref, in1_ref, in2_ref, in3_ref, question_ref, content_ref, down_ref, onehot_ref):
    width = question_ref.shape[1]
    rows = jnp.concatenate([own_ref[...], in1_ref[...], in2_ref[...], in3_ref[...]], axis=0)
    onehot = rows[:, width:]
    onehot_ref[...] = onehot
    onehot = onehot.astype(jnp.float32)
    left = lax.broadcasted_iota(jnp.int32, (rows.shape[0], 2 * rank), 1) < rank
    sums = []
    for weight_ref in (question_ref, content_ref):
        every = lax.dot_general(
            rows[:, :width],
            weight_ref[...],
            (((1,), (1,)), ((), ())),
            preferred_element_type=jnp.float32,
        )
        kept = 0.0
        for pair in range(voices // 2):
            mask = jnp.where(left, onehot[:, 2 * pair : 2 * pair + 1], onehot[:, 2 * pair + 1 : 2 * pair + 2])
            kept = kept + mask * every[:, 2 * pair * rank : 2 * (pair + 1) * rank]
        sums.append(kept[:, :rank] + kept[:, rank:])
    down_ref[...] = jnp.concatenate(sums, axis=1)


def lower(pieces, question, content, voices, rank):
    rows = sum(piece.shape[0] for piece in pieces)
    return pl.pallas_call(
        functools.partial(lowering_kernel, voices, rank),
        out_shape=(
            jax.ShapeDtypeStruct((rows, 2 * rank), jnp.float32),
            jax.ShapeDtypeStruct((rows, 128), jnp.bfloat16),
        ),
        cost_estimate=pl.CostEstimate(flops=1000, bytes_accessed=1000, transcendentals=0),
        compiler_params=pltpu.CompilerParams(vmem_limit_bytes=16 << 20),
    )(*pieces, question, content)


def per_device_four(
    tokens,
    attention_gain,
    query_weight,
    key_weight,
    value_weight,
    speaker_question_lowering,
    speaker_question_raising,
    speaker_content_lowering,
    speaker_content_raising,
    rotated_key_cache,
    stored_value_cache,
    sequence_speaker_label,
    lengths,
    output_weight,
    closing_gain,
    codebook_weight,
    delays,
):
    n_adapter = lax.axis_size("adapter")
    peers = range(1, n_adapter)
    a = lax.axis_index("adapter")
    t = lax.axis_index("tensor")
    core = t % 2
    str_dev, model_width = tokens.shape
    half = str_dev // 2
    d_slice = model_width // n_adapter
    voices, rank = speaker_question_raising.shape[:2]
    query_columns = query_weight.shape[1]
    key_value_columns = key_weight.shape[1]

    tok_f = tokens.astype(jnp.float32)
    inverse = lax.rsqrt(jnp.mean(tok_f * tok_f, axis=-1, keepdims=True) + NORM_EPS)
    normed = (tok_f * inverse * attention_gain).astype(jnp.bfloat16)

    my_half = take_block(normed, core, half)
    came = [swap(take_block(my_half, a ^ k, d_slice, 1), "adapter", k) for k in peers]

    slot_cap = max(2, 2 * str_dev // n_adapter)
    owner_ids = sequence_speaker_label // voices
    local_voice = sequence_speaker_label % voices
    same_owner = owner_ids[:, None] == owner_ids[None, :]
    earlier = jnp.arange(str_dev)[:, None] > jnp.arange(str_dev)[None, :]
    owner_rank = jnp.sum((same_owner & earlier).astype(jnp.int32), axis=1)
    slot_ids = (owner_ids ^ a) * slot_cap + owner_rank
    placing = (slot_ids[None, :] == jnp.arange(n_adapter * slot_cap)[:, None]).astype(jnp.bfloat16)
    voice_onehot = (local_voice[:, None] == jnp.arange(128)[None, :]).astype(jnp.bfloat16)
    sent_rows = jnp.dot(
        placing,
        jnp.concatenate([take_block(normed, t, d_slice, 1), voice_onehot], axis=1),
        preferred_element_type=jnp.float32,
    ).astype(jnp.bfloat16)
    rows_in = [sent_rows[:slot_cap]] + [
        swap(sent_rows[k * slot_cap : (k + 1) * slot_cap], "adapter", k) for k in peers
    ]

    came = jnp.stack(came)
    other = swap(came, "tensor", 1)
    first = jnp.where(core == 0, came, other)
    second = jnp.where(core == 0, other, came)
    arrived = jnp.concatenate([first, second], axis=1).reshape(-1, d_slice)
    norm_cols = jnp.concatenate([take_block(normed, a, d_slice, 1), arrived], axis=0)
    base = jnp.concatenate(
        [
            jnp.dot(norm_cols, weight, preferred_element_type=jnp.float32)
            for weight in (query_weight, key_weight, value_weight)
        ],
        axis=1,
    )

    base, rows_in = lax.optimization_barrier((base, rows_in))
    projected = base[:str_dev]
    for k in peers:
        projected = projected + swap(base[k * str_dev : (k + 1) * str_dev], "adapter", k)
    down, onehot = lower(
        rows_in,
        speaker_question_lowering.transpose(1, 2, 0).reshape(voices * rank, d_slice),
        speaker_content_lowering.transpose(1, 2, 0).reshape(voices * rank, d_slice),
        voices,
        rank,
    )
    onehot_b = onehot[:, :voices]
    down = down + swap(down, "tensor", 1)
    down = (down + swap(down, "tensor", 2)).astype(jnp.bfloat16)
    ups = []
    for i, raising in enumerate((speaker_question_raising, speaker_content_raising)):
        spread = (
            onehot_b[:, :, None] * down[:, None, i * rank : (i + 1) * rank]
        ).reshape(-1, voices * rank)
        up = jnp.dot(
            spread, raising.reshape(voices * rank, -1), preferred_element_type=jnp.float32
        )
        ups.append((up * ADAPTER_SCALE).astype(jnp.bfloat16))
    outgoing = jnp.concatenate(ups, axis=1)
    returned = jnp.concatenate(
        [outgoing[:slot_cap]]
        + [swap(outgoing[k * slot_cap : (k + 1) * slot_cap], "adapter", k) for k in peers],
        axis=0,
    )
    adapter_summands = jnp.einsum(
        "ms,mc->sc", placing, returned, preferred_element_type=jnp.float32
    )

    kv_local, ctx_len, head_dim = rotated_key_cache.shape[1:]
    group_size = query_columns // (kv_local * head_dim)
    query = rotate(
        (projected[:, :query_columns] + adapter_summands[:, :query_columns]).reshape(
            str_dev, kv_local, group_size, head_dim
        ),
        lengths,
    ).astype(jnp.bfloat16)
    key_base = projected[:, query_columns : query_columns + key_value_columns]
    key_new = rotate(key_base.reshape(str_dev, kv_local, head_dim), lengths).astype(jnp.bfloat16)
    value_new = (
        (projected[:, query_columns + key_value_columns :] + adapter_summands[:, query_columns:])
        .reshape(str_dev, kv_local, head_dim)
        .astype(jnp.bfloat16)
    )
    scale_factor = 1.0 / head_dim**0.5
    scores = (
        jnp.einsum("skgd,skcd->skgc", query, rotated_key_cache, preferred_element_type=jnp.float32)
        * scale_factor
    )
    own_score = (
        jnp.einsum("skgd,skd->skg", query, key_new, preferred_element_type=jnp.float32)
        * scale_factor
    )
    valid = (jnp.arange(ctx_len)[None, :] < lengths[:, None])[:, None, None, :]
    masked = jnp.where(valid, scores, -1e30)
    top_score = jnp.maximum(jnp.max(masked, axis=-1), own_score)
    weights_all = jnp.where(valid, jnp.exp(scores - top_score[..., None]), 0.0)
    own_weight = jnp.exp(own_score - top_score)
    total = jnp.sum(weights_all, axis=-1) + own_weight
    probs = (weights_all / total[..., None]).astype(jnp.bfloat16)
    own_prob = (own_weight / total).astype(jnp.bfloat16)
    mixed = jnp.einsum(
        "skgc,skcd->skgd", probs, stored_value_cache, preferred_element_type=jnp.float32
    )
    mixed = (
        mixed
        + own_prob.astype(jnp.float32)[..., None] * value_new.astype(jnp.float32)[:, :, None, :]
    )
    attended = mixed.astype(jnp.bfloat16).reshape(str_dev, query_columns)

    raw = lax.ppermute(
        take_block(tokens, t, d_slice, 1),
        ("adapter", "tensor"),
        [(i * n_adapter + j, j * n_adapter + i) for i in range(n_adapter) for j in range(n_adapter)],
    )
    gathered = jnp.concatenate(
        [attended] + [swap(attended, "adapter", k) for k in peers], axis=0
    )
    partial_out = jnp.dot(gathered, output_weight, preferred_element_type=jnp.float32)
    turn = a ^ t
    near = swap(
        jnp.concatenate(
            [take_block(partial_out, turn ^ 1, str_dev), take_block(partial_out, turn ^ 3, str_dev)]
        ),
        "tensor",
        1,
    )
    far = take_block(partial_out, turn ^ 2, str_dev) + near[str_dev:]
    summed_out = take_block(partial_out, turn, str_dev) + near[:str_dev] + swap(far, "tensor", 2)
    hidden_out = (raw.astype(jnp.float32) + summed_out).astype(jnp.bfloat16)

    hidden_f = hidden_out.astype(jnp.float32)
    square = jnp.sum(hidden_f * hidden_f, axis=-1)
    square_pair = jnp.stack([square, swap(square, "tensor", 2)])
    squares = jnp.concatenate([square_pair, swap(square_pair, "tensor", 1)]).reshape(-1)
    square_sum = squares
    for k in peers:
        square_sum = square_sum + swap(squares, "adapter", k)
    hidden_pair = jnp.concatenate([hidden_out, swap(hidden_out, "tensor", 2)])
    hidden_all = jnp.concatenate([hidden_pair, swap(hidden_pair, "tensor", 1)])
    final_slice = take_block(closing_gain, a, d_slice)
    final_normed = (
        hidden_all.astype(jnp.float32)
        * lax.rsqrt(square_sum / model_width + NORM_EPS)[:, None]
        * final_slice
    ).astype(jnp.bfloat16)

    books_local = CB // lax.axis_size("tensor")
    book_delays = take_block(delays, t, books_local)
    active = (lengths[:, None] >= book_delays[None, :]).astype(jnp.float32)
    place = jnp.array([0, 2, 1, 3], jnp.int32)
    parts = LOGIT_PARTS
    width = codebook_weight.shape[1] // parts
    outs = []
    for p in range(parts):
        partial = jnp.dot(
            final_normed,
            codebook_weight[:, p * width : (p + 1) * width],
            preferred_element_type=jnp.float32,
        )
        total_p = take_block(partial, place[turn], str_dev)
        for k in peers:
            block = take_block(partial, place[turn ^ k], str_dev)
            total_p = total_p + swap(
                (block * 32.0).astype(jnp.float16), "adapter", k
            ).astype(jnp.float32) * (1.0 / 32.0)
        outs.append(total_p)
    logits = jnp.concatenate(outs, axis=1).reshape(str_dev, books_local, VOC) * active[:, :, None]
    return (hidden_out, logits)


def per_device(
    tokens,
    attention_gain,
    query_weight,
    key_weight,
    value_weight,
    speaker_question_lowering,
    speaker_question_raising,
    speaker_content_lowering,
    speaker_content_raising,
    rotated_key_cache,
    stored_value_cache,
    sequence_speaker_label,
    lengths,
    output_weight,
    closing_gain,
    codebook_weight,
    delays,
):
    n_adapter = lax.axis_size("adapter")
    n_tensor = lax.axis_size("tensor")
    adapter_pos = lax.axis_index("adapter")
    tensor_pos = lax.axis_index("tensor")
    str_dev, model_width = tokens.shape
    all_streams = str_dev * n_adapter
    d_slice = model_width // n_adapter
    tensor_width = model_width // n_tensor
    tok_f = tokens.astype(jnp.float32)
    inverse = lax.rsqrt(jnp.mean(tok_f * tok_f, axis=-1, keepdims=True) + NORM_EPS)
    rescaled_hidden_state = (tok_f * inverse * attention_gain).astype(jnp.bfloat16)
    raw_cols, norm_cols = (
        lax.all_to_all(tokens, "adapter", split_axis=1, concat_axis=0, tiled=True),
        lax.all_to_all(rescaled_hidden_state, "adapter", split_axis=1, concat_axis=0, tiled=True),
    )
    query_columns = query_weight.shape[1]
    key_value_columns = key_weight.shape[1]
    weights_cat = jnp.concatenate([query_weight, key_weight, value_weight], axis=1)
    full_proj = jnp.dot(norm_cols, weights_cat, preferred_element_type=jnp.float32)
    summed = lax.psum(full_proj, "adapter")
    projected = lax.dynamic_slice_in_dim(summed, adapter_pos * str_dev, str_dev, 0)
    plain_query = projected[:, :query_columns]
    key_base = projected[:, query_columns : query_columns + key_value_columns]
    plain_value = projected[:, query_columns + key_value_columns :]
    voices_per_shard = speaker_question_raising.shape[0]
    adapter_rank_size = speaker_question_raising.shape[1]
    slot_cap = max(2, 2 * str_dev // n_adapter)
    slot_total = n_adapter * slot_cap
    owner_ids = sequence_speaker_label // voices_per_shard
    local_voice = sequence_speaker_label % voices_per_shard
    same_owner = owner_ids[:, None] == owner_ids[None, :]
    earlier = jnp.arange(str_dev)[:, None] > jnp.arange(str_dev)[None, :]
    owner_rank = jnp.sum((same_owner & earlier).astype(jnp.int32), axis=1)
    slot_ids = owner_ids * slot_cap + owner_rank
    placing = (slot_ids[None, :] == jnp.arange(slot_total)[:, None]).astype(jnp.bfloat16)
    voice_onehot = (local_voice[:, None] == jnp.arange(voices_per_shard)[None, :]).astype(
        jnp.bfloat16
    )
    normed_part = lax.dynamic_slice_in_dim(
        rescaled_hidden_state, tensor_pos * tensor_width, tensor_width, 1
    )
    send_rows = jnp.dot(placing, normed_part, preferred_element_type=jnp.float32).astype(
        jnp.bfloat16
    )
    send_voice = jnp.dot(placing, voice_onehot, preferred_element_type=jnp.float32).astype(
        jnp.bfloat16
    )
    send_rows = send_rows.reshape(n_adapter, slot_cap, tensor_width)
    send_voice = send_voice.reshape(n_adapter, slot_cap, voices_per_shard)
    query_down_matrix = speaker_question_lowering.reshape(
        tensor_width, voices_per_shard * adapter_rank_size
    )
    value_down_matrix = speaker_content_lowering.reshape(
        tensor_width, voices_per_shard * adapter_rank_size
    )
    query_up_matrix = speaker_question_raising.reshape(
        voices_per_shard * adapter_rank_size, query_columns
    )
    value_up_matrix = speaker_content_raising.reshape(
        voices_per_shard * adapter_rank_size, key_value_columns
    )
    rows_in = lax.all_to_all(send_rows, "adapter", split_axis=0, concat_axis=0, tiled=True)
    voices_in = lax.all_to_all(send_voice, "adapter", split_axis=0, concat_axis=0, tiled=True)
    item_count = rows_in.shape[1]
    flat_rows = rows_in.reshape(-1, tensor_width)
    onehot_b = voices_in.reshape(-1, voices_per_shard)
    onehot_f = onehot_b.astype(jnp.float32)
    all_q = jnp.dot(flat_rows, query_down_matrix, preferred_element_type=jnp.float32).reshape(
        -1, voices_per_shard, adapter_rank_size
    )
    all_v = jnp.dot(flat_rows, value_down_matrix, preferred_element_type=jnp.float32).reshape(
        -1, voices_per_shard, adapter_rank_size
    )
    down_q = jnp.sum(onehot_f[:, :, None] * all_q, axis=1)
    down_v = jnp.sum(onehot_f[:, :, None] * all_v, axis=1)
    down_q, down_v = lax.psum((down_q, down_v), "tensor")
    query_broadcast = (onehot_b[:, :, None] * down_q.astype(jnp.bfloat16)[:, None, :]).reshape(
        -1, voices_per_shard * adapter_rank_size
    )
    value_broadcast = (onehot_b[:, :, None] * down_v.astype(jnp.bfloat16)[:, None, :]).reshape(
        -1, voices_per_shard * adapter_rank_size
    )
    question_raised_product = (
        jnp.dot(query_broadcast, query_up_matrix, preferred_element_type=jnp.float32)
        * ADAPTER_SCALE
    ).astype(jnp.bfloat16)
    content_raised_product = (
        jnp.dot(value_broadcast, value_up_matrix, preferred_element_type=jnp.float32)
        * ADAPTER_SCALE
    ).astype(jnp.bfloat16)
    outgoing = jnp.concatenate([question_raised_product, content_raised_product], axis=1).reshape(
        n_adapter, item_count, query_columns + key_value_columns
    )
    returned = lax.all_to_all(outgoing, "adapter", split_axis=0, concat_axis=0, tiled=True)
    adapter_summands = jnp.einsum(
        "ms,mc->sc",
        placing,
        returned.reshape(slot_total, query_columns + key_value_columns),
        preferred_element_type=jnp.float32,
    )
    kv_local = rotated_key_cache.shape[1]
    head_dim = rotated_key_cache.shape[3]
    ctx_len = rotated_key_cache.shape[2]
    group_size = query_columns // (kv_local * head_dim)
    adapted_query = (plain_query + adapter_summands[:, :query_columns]).reshape(
        str_dev, kv_local, group_size, head_dim
    )
    query = rotate(adapted_query, lengths).astype(jnp.bfloat16)
    key_new = rotate(key_base.reshape(str_dev, kv_local, head_dim), lengths).astype(jnp.bfloat16)
    value_new = (
        (plain_value + adapter_summands[:, query_columns:])
        .reshape(str_dev, kv_local, head_dim)
        .astype(jnp.bfloat16)
    )
    scale_factor = 1.0 / head_dim**0.5
    scores = (
        jnp.einsum("skgd,skcd->skgc", query, rotated_key_cache, preferred_element_type=jnp.float32)
        * scale_factor
    )
    own_score = (
        jnp.einsum("skgd,skd->skg", query, key_new, preferred_element_type=jnp.float32)
        * scale_factor
    )
    valid = (jnp.arange(ctx_len)[None, :] < lengths[:, None])[:, None, None, :]
    masked = jnp.where(valid, scores, -1e30)
    top_score = jnp.maximum(jnp.max(masked, axis=-1), own_score)
    weights_all = jnp.where(valid, jnp.exp(scores - top_score[..., None]), 0.0)
    own_weight = jnp.exp(own_score - top_score)
    total = jnp.sum(weights_all, axis=-1) + own_weight
    probs = (weights_all / total[..., None]).astype(jnp.bfloat16)
    own_prob = (own_weight / total).astype(jnp.bfloat16)
    mixed = jnp.einsum(
        "skgc,skcd->skgd", probs, stored_value_cache, preferred_element_type=jnp.float32
    )
    mixed = (
        mixed
        + own_prob.astype(jnp.float32)[..., None] * value_new.astype(jnp.float32)[:, :, None, :]
    )
    attended = mixed.astype(jnp.bfloat16).reshape(str_dev, query_columns)
    partial_out = jnp.dot(
        lax.all_gather(attended, "adapter", axis=0, tiled=True),
        output_weight,
        preferred_element_type=jnp.float32,
    )
    final_slice = lax.dynamic_slice_in_dim(closing_gain, adapter_pos * d_slice, d_slice)
    rows_tensor = all_streams // n_tensor
    summed_out = lax.psum(partial_out, "tensor")
    hidden_all = (raw_cols.astype(jnp.float32) + summed_out).astype(jnp.bfloat16)
    hidden_f = hidden_all.astype(jnp.float32)
    square_sum = lax.psum(jnp.sum(hidden_f * hidden_f, axis=-1), "adapter")
    final_normed = (
        hidden_f * lax.rsqrt(square_sum / model_width + NORM_EPS)[:, None] * final_slice
    ).astype(jnp.bfloat16)
    hidden_out = lax.dynamic_slice_in_dim(hidden_all, tensor_pos * rows_tensor, rows_tensor, 0)
    logit_rows = lax.psum_scatter(
        jnp.dot(final_normed, codebook_weight, preferred_element_type=jnp.float32),
        "adapter",
        scatter_dimension=0,
        tiled=True,
    )
    books_local = CB // n_tensor
    book_delays = lax.dynamic_slice_in_dim(delays, tensor_pos * books_local, books_local)
    active = (lengths[:, None] >= book_delays[None, :]).astype(jnp.float32)
    logits = logit_rows.reshape(str_dev, books_local, VOC) * active[:, :, None]
    return (hidden_out, logits)


def solution(mesh):
    in_specs = (
        P(("groups", "adapter"), None),
        P(),
        P("adapter", "tensor"),
        P("adapter", "tensor"),
        P("adapter", "tensor"),
        P("tensor", "adapter", None),
        P("adapter", None, "tensor"),
        P("tensor", "adapter", None),
        P("adapter", None, "tensor"),
        P(("groups", "adapter"), "tensor", None, None),
        P(("groups", "adapter"), "tensor", None, None),
        P(("groups", "adapter")),
        P(("groups", "adapter")),
        P("tensor", "adapter"),
        P(),
        P("adapter", "tensor"),
        P(),
    )
    out_specs = (P(("groups", "tensor"), "adapter"), P(("groups", "adapter"), "tensor", None))
    four = mesh.shape["adapter"] == 4 and mesh.shape["tensor"] == 4
    return jax.shard_map(
        per_device_four if four else per_device, mesh=mesh, in_specs=in_specs, out_specs=out_specs, check_vma=False
    )
```

```python
import functools

import jax
import jax.numpy as jnp
from jax import lax
from jax.experimental import pallas as pl
from jax.experimental.pallas import tpu as pltpu
from jax.sharding import PartitionSpec as P

CB = 8
VOC = 2048


ROPE_BASE = 500000.0
NORM_EPS = 1e-05
ADAPTER_SCALE = 0.5
LOGIT_PARTS = 2
KERNEL_VMEM = 8 << 20


def rotate(values, positions):
    head_dim = values.shape[-1]
    half_dim = head_dim // 2
    spacing = jnp.arange(half_dim, dtype=jnp.float32) * (2.0 / head_dim)
    angles = positions.astype(jnp.float32)[:, None] * jnp.power(ROPE_BASE, -spacing)[None, :]
    new_shape = (values.shape[0],) + (1,) * (values.ndim - 2) + (half_dim,)
    cosine = jnp.cos(angles).reshape(new_shape)
    sine = jnp.sin(angles).reshape(new_shape)
    first_half = values[..., :half_dim]
    second_half = values[..., half_dim:]
    return jnp.concatenate(
        [first_half * cosine - second_half * sine, first_half * sine + second_half * cosine],
        axis=-1,
    )


def swap(value, axis, distance):
    size = lax.axis_size(axis)
    return lax.ppermute(value, axis, [(i, i ^ distance) for i in range(size)])


def take_block(array, index, size, axis=0):
    return lax.dynamic_slice_in_dim(array, index * size, size, axis)


def full_spec():
    return pl.BlockSpec(memory_space=pltpu.VMEM)


def call(kernel, outs, operands, scalars=(), scratch=(), resident=(), hbm=()):
    hbm = [pltpu.with_memory_space_constraint(array, pltpu.HBM) for array in hbm]
    resident = [pltpu.with_memory_space_constraint(array, pltpu.VMEM) for array in resident]
    specs = [pl.BlockSpec(memory_space=pl.ANY)] * len(hbm)
    specs += [full_spec()] * (len(operands) + len(resident))
    arrays = [*hbm, *operands, *resident]
    specs = [pl.BlockSpec(memory_space=pltpu.SMEM)] * len(scalars) + specs
    arrays = [*scalars, *arrays]
    return pl.pallas_call(
        kernel,
        out_shape=tuple(outs),
        in_specs=specs,
        out_specs=tuple(full_spec() for _ in outs),
        scratch_shapes=scratch,
        cost_estimate=pl.CostEstimate(flops=1000, bytes_accessed=1000, transcendentals=0),
        compiler_params=pltpu.CompilerParams(vmem_limit_bytes=KERNEL_VMEM),
    )(*arrays)


def shaped(shape, dtype):
    return jax.ShapeDtypeStruct(shape, dtype)


def norm_kernel(
    n_adapter, voices, books, place_ref, delays_ref, tokens_hbm, gain_hbm, label_hbm, lengths_hbm, closing_hbm,
    own_ref, rows_ref, out1_ref, out2_ref, out3_ref, placing_ref, raw_ref, active_ref, closing_ref,
    normed_ref, tokens_ref, gain_ref, label_ref, lengths_ref, sems,
):
    a, t = place_ref[0], place_ref[1]
    streams, model_width = tokens_ref.shape
    d_slice = own_ref.shape[1]
    closing_part = closing_hbm.at[:, pl.ds(pl.multiple_of(a * d_slice, d_slice), d_slice)]
    copies = [
        pltpu.make_async_copy(source, target, sems.at[i])
        for i, (source, target) in enumerate(
            (
                (tokens_hbm, tokens_ref),
                (gain_hbm, gain_ref),
                (label_hbm, label_ref),
                (lengths_hbm, lengths_ref),
                (closing_part, closing_ref),
            )
        )
    ]
    for copy in copies:
        copy.start()
    for copy in copies:
        copy.wait()
    half = streams // 2
    cap = rows_ref.shape[0]
    tok = tokens_ref[...].astype(jnp.float32)
    mean = jnp.sum(tok * tok, axis=-1, keepdims=True) * (1.0 / model_width)
    normed_ref[...] = (tok * lax.rsqrt(mean + NORM_EPS) * gain_ref[...]).astype(jnp.bfloat16)

    def owner_of(label):
        return sum((label >= j * voices).astype(jnp.int32) for j in range(1, n_adapter))

    square = (streams, streams)
    row_index = lax.broadcasted_iota(jnp.int32, square, 0)
    col_index = lax.broadcasted_iota(jnp.int32, square, 1)

    def column(row):
        picked = jnp.where(row_index == col_index, row.astype(jnp.float32), 0.0)
        return jnp.sum(picked, axis=1, keepdims=True).astype(jnp.int32)

    label_row = label_ref[...]
    label_col = column(label_row)
    owner_row, owner_col = owner_of(label_row), owner_of(label_col)
    voice = label_col - owner_col * voices
    earlier = (owner_col == owner_row) & (row_index < col_index)
    rank = jnp.sum(earlier.astype(jnp.float32), axis=0, keepdims=True).astype(jnp.int32)
    slot = jnp.bitwise_xor(owner_row, a) * cap + rank
    slots = (n_adapter * cap, streams)
    placing = (lax.broadcasted_iota(jnp.int32, slots, 0) == slot).astype(jnp.float32).astype(jnp.bfloat16)
    placing_ref[...] = placing
    lanes = (streams, 128)
    onehot = (lax.broadcasted_iota(jnp.int32, lanes, 1) == voice).astype(jnp.float32).astype(jnp.bfloat16)
    mine = normed_ref[:, pl.ds(pl.multiple_of(t * d_slice, d_slice), d_slice)]
    rows = jnp.dot(placing, mine, preferred_element_type=jnp.float32).astype(jnp.bfloat16)
    kinds = jnp.dot(placing, onehot, preferred_element_type=jnp.float32).astype(jnp.bfloat16)
    own_ref[...] = normed_ref[:, pl.ds(pl.multiple_of(a * d_slice, d_slice), d_slice)]
    rows_ref[:, :d_slice] = rows[:cap]
    rows_ref[:, d_slice:] = kinds[:cap]
    first = pl.multiple_of(lax.rem(t, 2) * half, half)
    length_col = column(lengths_ref[...])
    lane = lax.broadcasted_iota(jnp.int32, active_ref.shape, 1)
    active = jnp.zeros(active_ref.shape, jnp.float32)
    for p in range(books):
        started = (length_col >= delays_ref[t * books + p]).astype(jnp.float32)
        active = jnp.where(lane == p, started, active)
    active_ref[...] = active
    quarter = raw_ref.shape[2]
    for k in range(n_adapter):
        first_raw = pl.multiple_of(jnp.bitwise_xor(a, k) * d_slice + t * quarter, quarter)
        raw_ref[k] = tokens_ref[:, pl.ds(first_raw, quarter)]
    for k, out_ref in enumerate((out1_ref, out2_ref, out3_ref), 1):
        start = pl.multiple_of(jnp.bitwise_xor(a, k) * d_slice, d_slice)
        out_ref[:half, :d_slice] = normed_ref[pl.ds(first, half), pl.ds(start, d_slice)]
        out_ref[:half, d_slice:] = jnp.zeros((half, 128), jnp.bfloat16)
        out_ref[half:, :d_slice] = rows[k * cap : (k + 1) * cap]
        out_ref[half:, d_slice:] = kinds[k * cap : (k + 1) * cap]


def lowering_kernel(
    voices, rank, own_ref, in1_ref, in2_ref, in3_ref, question_ref, content_ref, down_ref, onehot_ref
):
    width = question_ref.shape[1]
    cap = own_ref.shape[0]
    rows = jnp.concatenate(
        [own_ref[...], in1_ref[cap:, :], in2_ref[cap:, :], in3_ref[cap:, :]], axis=0
    )
    onehot = rows[:, width:]
    onehot_ref[...] = onehot
    onehot = onehot.astype(jnp.float32)
    left = lax.broadcasted_iota(jnp.int32, (rows.shape[0], 2 * rank), 1) < rank
    sums = []
    for weight_ref in (question_ref, content_ref):
        every = lax.dot_general(
            rows[:, :width],
            weight_ref[...],
            (((1,), (1,)), ((), ())),
            preferred_element_type=jnp.float32,
        )
        kept = 0.0
        for pair in range(voices // 2):
            mask = jnp.where(left, onehot[:, 2 * pair : 2 * pair + 1], onehot[:, 2 * pair + 1 : 2 * pair + 2])
            kept = kept + mask * every[:, 2 * pair * rank : 2 * (pair + 1) * rank]
        sums.append(kept[:, :rank] + kept[:, rank:])
    down_ref[...] = jnp.concatenate(sums, axis=1)


def raising_kernel(
    voices, rank, near_ref, far_ref, onehot_ref, question_ref, content_ref,
    own_ref, out1_ref, out2_ref, out3_ref,
):
    down = (near_ref[...] + far_ref[...]).astype(jnp.bfloat16).astype(jnp.float32)
    onehot = onehot_ref[...].astype(jnp.float32)
    left = lax.broadcasted_iota(jnp.int32, (down.shape[0], 2 * rank), 1) < rank
    first = 0
    for i, weight_ref in enumerate((question_ref, content_ref)):
        part = down[:, i * rank : (i + 1) * rank]
        twice = jnp.concatenate([part, part], axis=1)
        spread = jnp.concatenate(
            [
                jnp.where(left, onehot[:, 2 * pair : 2 * pair + 1], onehot[:, 2 * pair + 1 : 2 * pair + 2])
                * twice
                for pair in range(voices // 2)
            ],
            axis=1,
        ).astype(jnp.bfloat16)
        up = jnp.dot(spread, weight_ref[...], preferred_element_type=jnp.float32) * ADAPTER_SCALE
        up = up.astype(jnp.bfloat16)
        last = first + weight_ref.shape[1]
        cap = own_ref.shape[0]
        for k, out_ref in enumerate((own_ref, out1_ref, out2_ref, out3_ref)):
            out_ref[:, first:last] = up[k * cap : (k + 1) * cap]
        first = last


def base_kernel(
    place_ref, own_ref, in1_ref, in2_ref, in3_ref, other_ref, query_ref, key_ref, value_ref,
    keep_ref, send_ref, rows_ref,
):
    core = lax.rem(place_ref[1], 2)
    streams, width = own_ref.shape
    half = streams // 2
    rows_ref[:streams, :] = own_ref[...]
    for k, in_ref in enumerate((in1_ref, in2_ref, in3_ref), 1):
        mine = pl.multiple_of(k * streams + core * half, half)
        theirs = pl.multiple_of(k * streams + (1 - core) * half, half)
        rows_ref[pl.ds(mine, half), :] = in_ref[:half, :width]
        rows_ref[pl.ds(theirs, half), :] = other_ref[(k - 1) * half : k * half, :]
    first = 0
    for weight_ref in (query_ref, key_ref, value_ref):
        last = first + weight_ref.shape[1]
        out = jnp.dot(rows_ref[...], weight_ref[...], preferred_element_type=jnp.float32)
        for k in range(4):
            out_ref = send_ref if k % 2 else keep_ref
            out_ref[k // 2 * streams : (k // 2 + 1) * streams, first:last] = out[
                k * streams : (k + 1) * streams
            ]
        first = last


def out_kernel(
    place_ref, own_ref, in1_ref, in2_ref, in3_ref, weight_ref, keep_ref, send_ref, rows_ref
):
    turn = jnp.bitwise_xor(place_ref[0], place_ref[1])
    streams = own_ref.shape[0]
    for k, in_ref in enumerate((own_ref, in1_ref, in2_ref, in3_ref)):
        first = pl.multiple_of(jnp.bitwise_xor(turn, k) * streams, streams)
        rows_ref[pl.ds(first, streams), :] = in_ref[...]
    depth = weight_ref.shape[0]
    quarter = rows_ref.shape[1] - depth
    column = pl.ds(pl.multiple_of(place_ref[1] * quarter, quarter), quarter)
    out = jnp.dot(rows_ref[:, :depth], weight_ref[...], preferred_element_type=jnp.float32)
    for m in range(4):
        out_ref = send_ref if m % 2 else keep_ref
        to, block = pl.ds(m // 2 * streams, streams), slice(m * streams, (m + 1) * streams)
        out_ref[to, :] = out[block]
        out_ref[to, column] += rows_ref[block, depth:].astype(jnp.float32)


def head_kernel(
    first, place_ref, own_ref, across_ref, pair_ref, scale_ref, gain_ref, weight_ref, out_ref, rows_ref
):
    turn = jnp.bitwise_xor(place_ref[0], place_ref[1])
    streams = own_ref.shape[0]
    diagonal = lax.broadcasted_iota(jnp.int32, (streams, streams), 0) == lax.broadcasted_iota(
        jnp.int32, (streams, streams), 1
    )
    pieces = (
        own_ref[...],
        pair_ref[:streams, :],
        across_ref[...],
        pair_ref[streams:, :],
    )
    for m, piece in enumerate(pieces):
        row = (0, 2, 1, 3)[m]
        scale = jnp.sum(
            jnp.where(diagonal, scale_ref[row : row + 1, :], 0.0), axis=1, keepdims=True
        )
        at = pl.multiple_of(jnp.bitwise_xor(turn, m) * streams, streams)
        rows_ref[pl.ds(at, streams), :] = (
            piece.astype(jnp.float32) * scale * gain_ref[...]
        ).astype(jnp.bfloat16)
    width = out_ref.shape[1]
    out_ref[...] = jnp.dot(
        rows_ref[...], weight_ref[:, first : first + width], preferred_element_type=jnp.float32
    )


def per_device_four(
    tokens,
    attention_gain,
    query_weight,
    key_weight,
    value_weight,
    speaker_question_lowering,
    speaker_question_raising,
    speaker_content_lowering,
    speaker_content_raising,
    rotated_key_cache,
    stored_value_cache,
    sequence_speaker_label,
    lengths,
    output_weight,
    closing_gain,
    codebook_weight,
    delays,
):
    n_adapter = lax.axis_size("adapter")
    peers = range(1, n_adapter)
    a = lax.axis_index("adapter")
    t = lax.axis_index("tensor")
    str_dev, model_width = tokens.shape
    place_ids = jnp.stack([a, t]).astype(jnp.int32)
    d_slice = model_width // n_adapter
    voices, rank = speaker_question_raising.shape[:2]
    query_columns = query_weight.shape[1]
    key_value_columns = key_weight.shape[1]

    bf16 = jnp.bfloat16
    slot_cap = max(2, 2 * str_dev // n_adapter)
    half = str_dev // 2
    n_tensor = lax.axis_size("tensor")
    quarter = d_slice // n_tensor
    books_local = CB // n_tensor
    own_cols, own_rows, *outgoing, placing, raw, active, final_slice = call(
        functools.partial(norm_kernel, n_adapter, voices, books_local),
        [shaped((str_dev, d_slice), bf16), shaped((slot_cap, d_slice + 128), bf16)]
        + [shaped((half + slot_cap, d_slice + 128), bf16)] * 3
        + [
            shaped((n_adapter * slot_cap, str_dev), bf16),
            shaped((n_adapter, str_dev, quarter), bf16),
            shaped((str_dev, 128), jnp.float32),
            shaped((1, d_slice), jnp.float32),
        ],
        [],
        [place_ids, delays],
        [
            pltpu.VMEM((str_dev, model_width), bf16),
            pltpu.VMEM((str_dev, model_width), bf16),
            pltpu.VMEM((1, model_width), jnp.float32),
            pltpu.VMEM((1, str_dev), jnp.int32),
            pltpu.VMEM((1, str_dev), jnp.int32),
            pltpu.SemaphoreType.DMA((5,)),
        ],
        hbm=[
            tokens,
            attention_gain[None],
            sequence_speaker_label[None],
            lengths[None],
            closing_gain[None],
        ],
    )
    came = [swap(payload, "adapter", k) for k, payload in zip(peers, outgoing)]
    other = swap(jnp.concatenate([piece[:half, :d_slice] for piece in came]), "tensor", 1)

    down, onehot = call(
        functools.partial(lowering_kernel, voices, rank),
        [shaped((n_adapter * slot_cap, 2 * rank), jnp.float32), shaped((n_adapter * slot_cap, 128), bf16)],
        [own_rows, *came],
        resident=[
            speaker_question_lowering.transpose(1, 2, 0).reshape(voices * rank, d_slice),
            speaker_content_lowering.transpose(1, 2, 0).reshape(voices * rank, d_slice),
        ],
    )
    other, down = lax.optimization_barrier((other, down))
    kept, sent = call(
        base_kernel,
        [shaped((2 * str_dev, query_columns + 2 * key_value_columns), jnp.float32)] * 2,
        [own_cols, *came, other],
        [place_ids],
        [pltpu.VMEM((n_adapter * str_dev, d_slice), bf16)],
        resident=[query_weight, key_weight, value_weight],
    )
    down = down + swap(down, "tensor", 1)
    summed = kept + swap(sent, "adapter", 1)
    raised = call(
        functools.partial(raising_kernel, voices, rank),
        [shaped((slot_cap, query_columns + key_value_columns), bf16)] * n_adapter,
        [down, swap(down, "tensor", 2), onehot],
        resident=[
            speaker_question_raising.reshape(voices * rank, query_columns),
            speaker_content_raising.reshape(voices * rank, key_value_columns),
        ],
    )
    returned = jnp.concatenate(
        [raised[0]] + [swap(raised[k], "adapter", k) for k in peers], axis=0
    )
    adapter_summands = jnp.einsum(
        "ms,mc->sc", placing, returned, preferred_element_type=jnp.float32
    )

    far = swap(summed[str_dev:], "adapter", 2)
    projected = summed[:str_dev] + far
    kv_local, ctx_len, head_dim = rotated_key_cache.shape[1:]
    group_size = query_columns // (kv_local * head_dim)
    query = rotate(
        (projected[:, :query_columns] + adapter_summands[:, :query_columns]).reshape(
            str_dev, kv_local, group_size, head_dim
        ),
        lengths,
    ).astype(jnp.bfloat16)
    key_base = projected[:, query_columns : query_columns + key_value_columns]
    key_new = rotate(key_base.reshape(str_dev, kv_local, head_dim), lengths).astype(jnp.bfloat16)
    value_new = (
        (projected[:, query_columns + key_value_columns :] + adapter_summands[:, query_columns:])
        .reshape(str_dev, kv_local, head_dim)
        .astype(jnp.bfloat16)
    )
    scale_factor = 1.0 / head_dim**0.5
    scores = (
        jnp.einsum("skgd,skcd->skgc", query, rotated_key_cache, preferred_element_type=jnp.float32)
        * scale_factor
    )
    own_score = (
        jnp.einsum("skgd,skd->skg", query, key_new, preferred_element_type=jnp.float32)
        * scale_factor
    )
    valid = (jnp.arange(ctx_len)[None, :] < lengths[:, None])[:, None, None, :]
    masked = jnp.where(valid, scores, -1e30)
    top_score = jnp.maximum(jnp.max(masked, axis=-1), own_score)
    weights_all = jnp.where(valid, jnp.exp(scores - top_score[..., None]), 0.0)
    own_weight = jnp.exp(own_score - top_score)
    total = jnp.sum(weights_all, axis=-1) + own_weight
    probs = (weights_all / total[..., None]).astype(jnp.bfloat16)
    own_prob = (own_weight / total).astype(jnp.bfloat16)
    mixed = jnp.einsum(
        "skgc,skcd->skgd", probs, stored_value_cache, preferred_element_type=jnp.float32
    )
    mixed = (
        mixed
        + own_prob.astype(jnp.float32)[..., None] * value_new.astype(jnp.float32)[:, :, None, :]
    )
    attended = mixed.astype(jnp.bfloat16).reshape(str_dev, query_columns)

    def with_raw(k):
        return jnp.concatenate([attended, raw[k]], axis=1)

    kept, sent = call(
        out_kernel,
        [shaped((2 * str_dev, d_slice), jnp.float32)] * 2,
        [with_raw(0)] + [swap(with_raw(k), "adapter", k) for k in peers],
        [place_ids],
        [pltpu.VMEM((n_adapter * str_dev, query_columns + quarter), bf16)],
        resident=[output_weight],
    )
    pair = kept + swap(sent, "tensor", 1)
    summed_out = pair[:str_dev] + swap(pair[str_dev:], "tensor", 2)
    hidden_out = summed_out.astype(jnp.bfloat16)

    hidden_f = hidden_out.astype(jnp.float32)
    square = jnp.sum(hidden_f * hidden_f, axis=-1)
    square_sum = square
    for k in peers:
        square_sum = square_sum + swap(square, "adapter", k)
    scale = lax.rsqrt(square_sum / model_width + NORM_EPS)[None]
    across = swap(hidden_out, "tensor", 2)
    hidden_pair = swap(jnp.concatenate([hidden_out, across]), "tensor", 1)
    scale = jnp.concatenate([scale, swap(scale, "tensor", 2)])
    scale = jnp.concatenate([scale, swap(scale, "tensor", 1)])

    width = codebook_weight.shape[1] // LOGIT_PARTS
    outs = []
    for p in range(LOGIT_PARTS):
        partial = call(
            functools.partial(head_kernel, p * width),
            [shaped((n_adapter * str_dev, width), jnp.float32)],
            [hidden_out, across, hidden_pair, scale, final_slice],
            [place_ids],
            [pltpu.VMEM((n_adapter * str_dev, d_slice), bf16)],
            resident=[codebook_weight],
        )[0]
        total_p = partial[:str_dev]
        for k in peers:
            block = partial[k * str_dev : (k + 1) * str_dev]
            total_p = total_p + swap(
                (block * 32.0).astype(jnp.float16), "adapter", k
            ).astype(jnp.float32) * (1.0 / 32.0)
        outs.append(total_p)
    if width == VOC:
        logits = jnp.stack([out * active[:, p : p + 1] for p, out in enumerate(outs)], axis=1)
    else:
        logits = jnp.concatenate(outs, axis=1).reshape(str_dev, books_local, VOC)
        logits = logits * active[:, :books_local, None]
    return (hidden_out, logits)


def per_device(
    tokens,
    attention_gain,
    query_weight,
    key_weight,
    value_weight,
    speaker_question_lowering,
    speaker_question_raising,
    speaker_content_lowering,
    speaker_content_raising,
    rotated_key_cache,
    stored_value_cache,
    sequence_speaker_label,
    lengths,
    output_weight,
    closing_gain,
    codebook_weight,
    delays,
):
    n_adapter = lax.axis_size("adapter")
    n_tensor = lax.axis_size("tensor")
    adapter_pos = lax.axis_index("adapter")
    tensor_pos = lax.axis_index("tensor")
    str_dev, model_width = tokens.shape
    all_streams = str_dev * n_adapter
    d_slice = model_width // n_adapter
    tensor_width = model_width // n_tensor
    tok_f = tokens.astype(jnp.float32)
    inverse = lax.rsqrt(jnp.mean(tok_f * tok_f, axis=-1, keepdims=True) + NORM_EPS)
    rescaled_hidden_state = (tok_f * inverse * attention_gain).astype(jnp.bfloat16)
    raw_cols, norm_cols = (
        lax.all_to_all(tokens, "adapter", split_axis=1, concat_axis=0, tiled=True),
        lax.all_to_all(rescaled_hidden_state, "adapter", split_axis=1, concat_axis=0, tiled=True),
    )
    query_columns = query_weight.shape[1]
    key_value_columns = key_weight.shape[1]
    weights_cat = jnp.concatenate([query_weight, key_weight, value_weight], axis=1)
    full_proj = jnp.dot(norm_cols, weights_cat, preferred_element_type=jnp.float32)
    summed = lax.psum(full_proj, "adapter")
    projected = lax.dynamic_slice_in_dim(summed, adapter_pos * str_dev, str_dev, 0)
    plain_query = projected[:, :query_columns]
    key_base = projected[:, query_columns : query_columns + key_value_columns]
    plain_value = projected[:, query_columns + key_value_columns :]
    voices_per_shard = speaker_question_raising.shape[0]
    adapter_rank_size = speaker_question_raising.shape[1]
    slot_cap = max(2, 2 * str_dev // n_adapter)
    slot_total = n_adapter * slot_cap
    owner_ids = sequence_speaker_label // voices_per_shard
    local_voice = sequence_speaker_label % voices_per_shard
    same_owner = owner_ids[:, None] == owner_ids[None, :]
    earlier = jnp.arange(str_dev)[:, None] > jnp.arange(str_dev)[None, :]
    owner_rank = jnp.sum((same_owner & earlier).astype(jnp.int32), axis=1)
    slot_ids = owner_ids * slot_cap + owner_rank
    placing = (slot_ids[None, :] == jnp.arange(slot_total)[:, None]).astype(jnp.bfloat16)
    voice_onehot = (local_voice[:, None] == jnp.arange(voices_per_shard)[None, :]).astype(
        jnp.bfloat16
    )
    normed_part = lax.dynamic_slice_in_dim(
        rescaled_hidden_state, tensor_pos * tensor_width, tensor_width, 1
    )
    send_rows = jnp.dot(placing, normed_part, preferred_element_type=jnp.float32).astype(
        jnp.bfloat16
    )
    send_voice = jnp.dot(placing, voice_onehot, preferred_element_type=jnp.float32).astype(
        jnp.bfloat16
    )
    send_rows = send_rows.reshape(n_adapter, slot_cap, tensor_width)
    send_voice = send_voice.reshape(n_adapter, slot_cap, voices_per_shard)
    query_down_matrix = speaker_question_lowering.reshape(
        tensor_width, voices_per_shard * adapter_rank_size
    )
    value_down_matrix = speaker_content_lowering.reshape(
        tensor_width, voices_per_shard * adapter_rank_size
    )
    query_up_matrix = speaker_question_raising.reshape(
        voices_per_shard * adapter_rank_size, query_columns
    )
    value_up_matrix = speaker_content_raising.reshape(
        voices_per_shard * adapter_rank_size, key_value_columns
    )
    rows_in = lax.all_to_all(send_rows, "adapter", split_axis=0, concat_axis=0, tiled=True)
    voices_in = lax.all_to_all(send_voice, "adapter", split_axis=0, concat_axis=0, tiled=True)
    item_count = rows_in.shape[1]
    flat_rows = rows_in.reshape(-1, tensor_width)
    onehot_b = voices_in.reshape(-1, voices_per_shard)
    onehot_f = onehot_b.astype(jnp.float32)
    all_q = jnp.dot(flat_rows, query_down_matrix, preferred_element_type=jnp.float32).reshape(
        -1, voices_per_shard, adapter_rank_size
    )
    all_v = jnp.dot(flat_rows, value_down_matrix, preferred_element_type=jnp.float32).reshape(
        -1, voices_per_shard, adapter_rank_size
    )
    down_q = jnp.sum(onehot_f[:, :, None] * all_q, axis=1)
    down_v = jnp.sum(onehot_f[:, :, None] * all_v, axis=1)
    down_q, down_v = lax.psum((down_q, down_v), "tensor")
    query_broadcast = (onehot_b[:, :, None] * down_q.astype(jnp.bfloat16)[:, None, :]).reshape(
        -1, voices_per_shard * adapter_rank_size
    )
    value_broadcast = (onehot_b[:, :, None] * down_v.astype(jnp.bfloat16)[:, None, :]).reshape(
        -1, voices_per_shard * adapter_rank_size
    )
    question_raised_product = (
        jnp.dot(query_broadcast, query_up_matrix, preferred_element_type=jnp.float32)
        * ADAPTER_SCALE
    ).astype(jnp.bfloat16)
    content_raised_product = (
        jnp.dot(value_broadcast, value_up_matrix, preferred_element_type=jnp.float32)
        * ADAPTER_SCALE
    ).astype(jnp.bfloat16)
    outgoing = jnp.concatenate([question_raised_product, content_raised_product], axis=1).reshape(
        n_adapter, item_count, query_columns + key_value_columns
    )
    returned = lax.all_to_all(outgoing, "adapter", split_axis=0, concat_axis=0, tiled=True)
    adapter_summands = jnp.einsum(
        "ms,mc->sc",
        placing,
        returned.reshape(slot_total, query_columns + key_value_columns),
        preferred_element_type=jnp.float32,
    )
    kv_local = rotated_key_cache.shape[1]
    head_dim = rotated_key_cache.shape[3]
    ctx_len = rotated_key_cache.shape[2]
    group_size = query_columns // (kv_local * head_dim)
    adapted_query = (plain_query + adapter_summands[:, :query_columns]).reshape(
        str_dev, kv_local, group_size, head_dim
    )
    query = rotate(adapted_query, lengths).astype(jnp.bfloat16)
    key_new = rotate(key_base.reshape(str_dev, kv_local, head_dim), lengths).astype(jnp.bfloat16)
    value_new = (
        (plain_value + adapter_summands[:, query_columns:])
        .reshape(str_dev, kv_local, head_dim)
        .astype(jnp.bfloat16)
    )
    scale_factor = 1.0 / head_dim**0.5
    scores = (
        jnp.einsum("skgd,skcd->skgc", query, rotated_key_cache, preferred_element_type=jnp.float32)
        * scale_factor
    )
    own_score = (
        jnp.einsum("skgd,skd->skg", query, key_new, preferred_element_type=jnp.float32)
        * scale_factor
    )
    valid = (jnp.arange(ctx_len)[None, :] < lengths[:, None])[:, None, None, :]
    masked = jnp.where(valid, scores, -1e30)
    top_score = jnp.maximum(jnp.max(masked, axis=-1), own_score)
    weights_all = jnp.where(valid, jnp.exp(scores - top_score[..., None]), 0.0)
    own_weight = jnp.exp(own_score - top_score)
    total = jnp.sum(weights_all, axis=-1) + own_weight
    probs = (weights_all / total[..., None]).astype(jnp.bfloat16)
    own_prob = (own_weight / total).astype(jnp.bfloat16)
    mixed = jnp.einsum(
        "skgc,skcd->skgd", probs, stored_value_cache, preferred_element_type=jnp.float32
    )
    mixed = (
        mixed
        + own_prob.astype(jnp.float32)[..., None] * value_new.astype(jnp.float32)[:, :, None, :]
    )
    attended = mixed.astype(jnp.bfloat16).reshape(str_dev, query_columns)
    partial_out = jnp.dot(
        lax.all_gather(attended, "adapter", axis=0, tiled=True),
        output_weight,
        preferred_element_type=jnp.float32,
    )
    final_slice = lax.dynamic_slice_in_dim(closing_gain, adapter_pos * d_slice, d_slice)
    rows_tensor = all_streams // n_tensor
    summed_out = lax.psum(partial_out, "tensor")
    hidden_all = (raw_cols.astype(jnp.float32) + summed_out).astype(jnp.bfloat16)
    hidden_f = hidden_all.astype(jnp.float32)
    square_sum = lax.psum(jnp.sum(hidden_f * hidden_f, axis=-1), "adapter")
    final_normed = (
        hidden_f * lax.rsqrt(square_sum / model_width + NORM_EPS)[:, None] * final_slice
    ).astype(jnp.bfloat16)
    hidden_out = lax.dynamic_slice_in_dim(hidden_all, tensor_pos * rows_tensor, rows_tensor, 0)
    logit_rows = lax.psum_scatter(
        jnp.dot(final_normed, codebook_weight, preferred_element_type=jnp.float32),
        "adapter",
        scatter_dimension=0,
        tiled=True,
    )
    books_local = CB // n_tensor
    book_delays = lax.dynamic_slice_in_dim(delays, tensor_pos * books_local, books_local)
    active = (lengths[:, None] >= book_delays[None, :]).astype(jnp.float32)
    logits = logit_rows.reshape(str_dev, books_local, VOC) * active[:, :, None]
    return (hidden_out, logits)


def solution(mesh):
    in_specs = (
        P(("groups", "adapter"), None),
        P(),
        P("adapter", "tensor"),
        P("adapter", "tensor"),
        P("adapter", "tensor"),
        P("tensor", "adapter", None),
        P("adapter", None, "tensor"),
        P("tensor", "adapter", None),
        P("adapter", None, "tensor"),
        P(("groups", "adapter"), "tensor", None, None),
        P(("groups", "adapter"), "tensor", None, None),
        P(("groups", "adapter")),
        P(("groups", "adapter")),
        P("tensor", "adapter"),
        P(),
        P("adapter", "tensor"),
        P(),
    )
    out_specs = (P(("groups", "tensor"), "adapter"), P(("groups", "adapter"), "tensor", None))
    four = mesh.shape["adapter"] == 4 and mesh.shape["tensor"] == 4
    return jax.shard_map(
        per_device_four if four else per_device, mesh=mesh, in_specs=in_specs, out_specs=out_specs, check_vma=False
    )
```

```python
import functools

import jax
import jax.numpy as jnp
from jax import lax
from jax.experimental import pallas as pl
from jax.experimental.pallas import tpu as pltpu
from jax.sharding import PartitionSpec as P

CB = 8
VOC = 2048


ROPE_BASE = 500000.0
NORM_EPS = 1e-05
ADAPTER_SCALE = 0.5
KERNEL_VMEM = 8 << 20


def rotate(values, positions):
    head_dim = values.shape[-1]
    half_dim = head_dim // 2
    spacing = jnp.arange(half_dim, dtype=jnp.float32) * (2.0 / head_dim)
    angles = positions.astype(jnp.float32)[:, None] * jnp.power(ROPE_BASE, -spacing)[None, :]
    new_shape = (values.shape[0],) + (1,) * (values.ndim - 2) + (half_dim,)
    cosine = jnp.cos(angles).reshape(new_shape)
    sine = jnp.sin(angles).reshape(new_shape)
    first_half = values[..., :half_dim]
    second_half = values[..., half_dim:]
    return jnp.concatenate(
        [first_half * cosine - second_half * sine, first_half * sine + second_half * cosine],
        axis=-1,
    )


def swap(value, axis, distance):
    size = lax.axis_size(axis)
    return lax.ppermute(value, axis, [(i, i ^ distance) for i in range(size)])


def take_block(array, index, size, axis=0):
    return lax.dynamic_slice_in_dim(array, index * size, size, axis)


def full_spec():
    return pl.BlockSpec(memory_space=pltpu.VMEM)


def call(kernel, outs, operands, scalars=(), scratch=(), resident=(), hbm=(), anywhere=()):
    hbm = [pltpu.with_memory_space_constraint(array, pltpu.HBM) for array in hbm]
    resident = [pltpu.with_memory_space_constraint(array, pltpu.VMEM) for array in resident]
    hbm += anywhere
    specs = [pl.BlockSpec(memory_space=pl.ANY)] * len(hbm)
    specs += [full_spec()] * (len(operands) + len(resident))
    arrays = [*hbm, *operands, *resident]
    specs = [pl.BlockSpec(memory_space=pltpu.SMEM)] * len(scalars) + specs
    arrays = [*scalars, *arrays]
    return pl.pallas_call(
        kernel,
        out_shape=tuple(outs),
        in_specs=specs,
        out_specs=tuple(full_spec() for _ in outs),
        scratch_shapes=scratch,
        cost_estimate=pl.CostEstimate(flops=1000, bytes_accessed=1000, transcendentals=0),
        compiler_params=pltpu.CompilerParams(vmem_limit_bytes=KERNEL_VMEM),
    )(*arrays)


def shaped(shape, dtype):
    return jax.ShapeDtypeStruct(shape, dtype)


def norm_kernel(
    n_adapter, voices, books, place_ref,
    tokens_hbm, gain_hbm, label_hbm, lengths_hbm, closing_hbm, delays_hbm,
    own_ref, rows_ref, out1_ref, out2_ref, out3_ref, placing_ref, raw_ref, active_ref, closing_ref,
    normed_ref, tokens_ref, gain_ref, label_ref, lengths_ref, delays_ref, sems,
):
    a, t = place_ref[0], place_ref[1]
    streams, model_width = tokens_ref.shape
    d_slice = own_ref.shape[1]
    closing_part = closing_hbm.at[:, pl.ds(pl.multiple_of(a * d_slice, d_slice), d_slice)]
    copies = [
        pltpu.make_async_copy(source, target, sems.at[i])
        for i, (source, target) in enumerate(
            (
                (tokens_hbm, tokens_ref),
                (gain_hbm, gain_ref),
                (label_hbm, label_ref),
                (lengths_hbm, lengths_ref),
                (closing_part, closing_ref),
                (delays_hbm, delays_ref),
            )
        )
    ]
    for copy in copies:
        copy.start()
    for copy in copies:
        copy.wait()
    half = streams // 2
    cap = rows_ref.shape[0]
    tok = tokens_ref[...].astype(jnp.float32)
    mean = jnp.sum(tok * tok, axis=-1, keepdims=True) * (1.0 / model_width)
    normed_ref[...] = (tok * lax.rsqrt(mean + NORM_EPS) * gain_ref[...]).astype(jnp.bfloat16)

    def owner_of(label):
        return sum((label >= j * voices).astype(jnp.int32) for j in range(1, n_adapter))

    square = (streams, streams)
    row_index = lax.broadcasted_iota(jnp.int32, square, 0)
    col_index = lax.broadcasted_iota(jnp.int32, square, 1)

    def column(row):
        picked = jnp.where(row_index == col_index, row.astype(jnp.float32), 0.0)
        return jnp.sum(picked, axis=1, keepdims=True).astype(jnp.int32)

    label_row = label_ref[...]
    label_col = column(label_row)
    owner_row, owner_col = owner_of(label_row), owner_of(label_col)
    voice = label_col - owner_col * voices
    earlier = (owner_col == owner_row) & (row_index < col_index)
    rank = jnp.sum(earlier.astype(jnp.float32), axis=0, keepdims=True).astype(jnp.int32)
    slot = jnp.bitwise_xor(owner_row, a) * cap + rank
    slots = (n_adapter * cap, streams)
    placing = (lax.broadcasted_iota(jnp.int32, slots, 0) == slot).astype(jnp.float32).astype(jnp.bfloat16)
    placing_ref[...] = placing
    lanes = (streams, 128)
    onehot = (lax.broadcasted_iota(jnp.int32, lanes, 1) == voice).astype(jnp.float32).astype(jnp.bfloat16)
    mine = normed_ref[:, pl.ds(pl.multiple_of(t * d_slice, d_slice), d_slice)]
    rows = jnp.dot(placing, mine, preferred_element_type=jnp.float32).astype(jnp.bfloat16)
    kinds = jnp.dot(placing, onehot, preferred_element_type=jnp.float32).astype(jnp.bfloat16)
    own_ref[...] = normed_ref[:, pl.ds(pl.multiple_of(a * d_slice, d_slice), d_slice)]
    rows_ref[:, :d_slice] = rows[:cap]
    rows_ref[:, d_slice:] = kinds[:cap]
    first = pl.multiple_of(lax.rem(t, 2) * half, half)
    length_col = column(lengths_ref[...])
    lane = lax.broadcasted_iota(jnp.int32, active_ref.shape, 1)
    active = jnp.zeros(active_ref.shape, jnp.float32)
    books_row = delays_ref[...].astype(jnp.float32)
    book = lax.broadcasted_iota(jnp.int32, books_row.shape, 1)
    for p in range(books):
        mine_only = jnp.where(book == t * books + p, books_row, 0.0)
        delay = jnp.sum(mine_only, axis=1, keepdims=True).astype(jnp.int32)
        started = (length_col >= delay).astype(jnp.float32)
        active = jnp.where(lane == p, started, active)
    active_ref[...] = active
    quarter = raw_ref.shape[2]
    for k in range(n_adapter):
        first_raw = pl.multiple_of(jnp.bitwise_xor(a, k) * d_slice + t * quarter, quarter)
        raw_ref[k] = tokens_ref[:, pl.ds(first_raw, quarter)]
    for k, out_ref in enumerate((out1_ref, out2_ref, out3_ref), 1):
        start = pl.multiple_of(jnp.bitwise_xor(a, k) * d_slice, d_slice)
        out_ref[:half, :d_slice] = normed_ref[pl.ds(first, half), pl.ds(start, d_slice)]
        out_ref[:half, d_slice:] = jnp.zeros((half, 128), jnp.bfloat16)
        out_ref[half:, :d_slice] = rows[k * cap : (k + 1) * cap]
        out_ref[half:, d_slice:] = kinds[k * cap : (k + 1) * cap]


def fetch_kernel(question_hbm, content_hbm, after_hbm, question_ref, content_ref, sems):
    copies = []
    for source, target in ((question_hbm, question_ref), (content_hbm, content_ref)):
        rows = source.shape[0] // 4
        for i in range(4):
            part = pl.ds(i * rows, rows)
            copies.append(
                pltpu.make_async_copy(source.at[part], target.at[part], sems.at[len(copies)])
            )
    for copy in copies:
        copy.start()
    for copy in copies:
        copy.wait()


def lowering_kernel(
    voices, rank, own_ref, in1_ref, in2_ref, in3_ref, question_ref, content_ref, down_ref, onehot_ref
):
    width = question_ref.shape[1]
    cap = own_ref.shape[0]
    rows = jnp.concatenate(
        [own_ref[...], in1_ref[cap:, :], in2_ref[cap:, :], in3_ref[cap:, :]], axis=0
    )
    onehot = rows[:, width:]
    onehot_ref[...] = onehot
    onehot = onehot.astype(jnp.float32)
    left = lax.broadcasted_iota(jnp.int32, (rows.shape[0], 2 * rank), 1) < rank
    sums = []
    for weight_ref in (question_ref, content_ref):
        every = lax.dot_general(
            rows[:, :width],
            weight_ref[...],
            (((1,), (1,)), ((), ())),
            preferred_element_type=jnp.float32,
        )
        kept = 0.0
        for pair in range(voices // 2):
            mask = jnp.where(left, onehot[:, 2 * pair : 2 * pair + 1], onehot[:, 2 * pair + 1 : 2 * pair + 2])
            kept = kept + mask * every[:, 2 * pair * rank : 2 * (pair + 1) * rank]
        sums.append(kept[:, :rank] + kept[:, rank:])
    down_ref[...] = jnp.concatenate(sums, axis=1)


def raising_kernel(
    voices, rank, near_ref, far_ref, onehot_ref, question_ref, content_ref,
    own_ref, out1_ref, out2_ref, out3_ref,
):
    down = (near_ref[...] + far_ref[...]).astype(jnp.bfloat16).astype(jnp.float32)
    onehot = onehot_ref[...].astype(jnp.float32)
    left = lax.broadcasted_iota(jnp.int32, (down.shape[0], 2 * rank), 1) < rank
    first = 0
    for i, weight_ref in enumerate((question_ref, content_ref)):
        part = down[:, i * rank : (i + 1) * rank]
        twice = jnp.concatenate([part, part], axis=1)
        spread = jnp.concatenate(
            [
                jnp.where(left, onehot[:, 2 * pair : 2 * pair + 1], onehot[:, 2 * pair + 1 : 2 * pair + 2])
                * twice
                for pair in range(voices // 2)
            ],
            axis=1,
        ).astype(jnp.bfloat16)
        up = jnp.dot(spread, weight_ref[...], preferred_element_type=jnp.float32) * ADAPTER_SCALE
        up = up.astype(jnp.bfloat16)
        last = first + weight_ref.shape[1]
        cap = own_ref.shape[0]
        for k, out_ref in enumerate((own_ref, out1_ref, out2_ref, out3_ref)):
            out_ref[:, first:last] = up[k * cap : (k + 1) * cap]
        first = last


def base_kernel(
    place_ref, own_ref, in1_ref, in2_ref, in3_ref, other_ref, query_ref, key_ref, value_ref,
    keep_ref, send_ref, rows_ref,
):
    core = lax.rem(place_ref[1], 2)
    streams, width = own_ref.shape
    half = streams // 2
    rows_ref[:streams, :] = own_ref[...]
    for k, in_ref in enumerate((in1_ref, in2_ref, in3_ref), 1):
        mine = pl.multiple_of(k * streams + core * half, half)
        theirs = pl.multiple_of(k * streams + (1 - core) * half, half)
        rows_ref[pl.ds(mine, half), :] = in_ref[:half, :width]
        rows_ref[pl.ds(theirs, half), :] = other_ref[(k - 1) * half : k * half, :]
    first = 0
    for weight_ref in (query_ref, key_ref, value_ref):
        last = first + weight_ref.shape[1]
        out = jnp.dot(rows_ref[...], weight_ref[...], preferred_element_type=jnp.float32)
        for k in range(4):
            out_ref = send_ref if k % 2 else keep_ref
            out_ref[k // 2 * streams : (k // 2 + 1) * streams, first:last] = out[
                k * streams : (k + 1) * streams
            ]
        first = last


def out_kernel(
    place_ref, own_ref, in1_ref, in2_ref, in3_ref, weight_ref, keep_ref, send_ref, rows_ref
):
    turn = jnp.bitwise_xor(place_ref[0], place_ref[1])
    streams = own_ref.shape[0]
    for k, in_ref in enumerate((own_ref, in1_ref, in2_ref, in3_ref)):
        first = pl.multiple_of(jnp.bitwise_xor(turn, k) * streams, streams)
        rows_ref[pl.ds(first, streams), :] = in_ref[...]
    depth = weight_ref.shape[0]
    quarter = rows_ref.shape[1] - depth
    column = pl.ds(pl.multiple_of(place_ref[1] * quarter, quarter), quarter)
    out = jnp.dot(rows_ref[:, :depth], weight_ref[...], preferred_element_type=jnp.float32)
    for m in range(4):
        out_ref = send_ref if m % 2 else keep_ref
        to, block = pl.ds(m // 2 * streams, streams), slice(m * streams, (m + 1) * streams)
        out_ref[to, :] = out[block]
        out_ref[to, column] += rows_ref[block, depth:].astype(jnp.float32)


def head_kernel(
    first, place_ref, own_ref, across_ref, pair_ref, scale_ref, gain_ref, weight_ref, keep_ref, send_ref, rows_ref
):
    turn = jnp.bitwise_xor(place_ref[0], place_ref[1])
    streams = own_ref.shape[0]
    diagonal = lax.broadcasted_iota(jnp.int32, (streams, streams), 0) == lax.broadcasted_iota(
        jnp.int32, (streams, streams), 1
    )
    pieces = (
        own_ref[...],
        pair_ref[:streams, :],
        across_ref[...],
        pair_ref[streams:, :],
    )
    for m, piece in enumerate(pieces):
        row = (0, 2, 1, 3)[m]
        scale = jnp.sum(
            jnp.where(diagonal, scale_ref[row : row + 1, :], 0.0), axis=1, keepdims=True
        )
        at = pl.multiple_of(jnp.bitwise_xor(turn, m) * streams, streams)
        rows_ref[pl.ds(at, streams), :] = (
            piece.astype(jnp.float32) * scale * gain_ref[...]
        ).astype(jnp.bfloat16)
    width = keep_ref.shape[1]
    out = 16.0 * jnp.dot(
        rows_ref[...], weight_ref[:, first : first + width], preferred_element_type=jnp.float32
    )
    keep_ref[:streams] = out[:streams]
    send_ref[:streams] = out[streams : 2 * streams]
    keep_ref[streams:] = out[2 * streams : 3 * streams]
    send_ref[streams:] = out[3 * streams :]


def per_device_four(
    tokens,
    attention_gain,
    query_weight,
    key_weight,
    value_weight,
    speaker_question_lowering,
    speaker_question_raising,
    speaker_content_lowering,
    speaker_content_raising,
    rotated_key_cache,
    stored_value_cache,
    sequence_speaker_label,
    lengths,
    output_weight,
    closing_gain,
    codebook_weight,
    delays,
):
    n_adapter = lax.axis_size("adapter")
    peers = range(1, n_adapter)
    a = lax.axis_index("adapter")
    t = lax.axis_index("tensor")
    str_dev, model_width = tokens.shape
    place_ids = jnp.stack([a, t]).astype(jnp.int32)
    d_slice = model_width // n_adapter
    voices, rank = speaker_question_raising.shape[:2]
    query_columns = query_weight.shape[1]
    key_value_columns = key_weight.shape[1]

    bf16 = jnp.bfloat16
    slot_cap = max(2, 2 * str_dev // n_adapter)
    half = str_dev // 2
    n_tensor = lax.axis_size("tensor")
    quarter = d_slice // n_tensor
    books_local = CB // n_tensor
    own_cols, own_rows, *outgoing, placing, raw, active, final_slice = call(
        functools.partial(norm_kernel, n_adapter, voices, books_local),
        [shaped((str_dev, d_slice), bf16), shaped((slot_cap, d_slice + 128), bf16)]
        + [shaped((half + slot_cap, d_slice + 128), bf16)] * 3
        + [
            shaped((n_adapter * slot_cap, str_dev), bf16),
            shaped((n_adapter, str_dev, quarter), bf16),
            shaped((str_dev, 128), jnp.float32),
            shaped((1, d_slice), jnp.float32),
        ],
        [],
        [place_ids],
        [
            pltpu.VMEM((str_dev, model_width), bf16),
            pltpu.VMEM((str_dev, model_width), bf16),
            pltpu.VMEM((1, model_width), jnp.float32),
            pltpu.VMEM((1, str_dev), jnp.int32),
            pltpu.VMEM((1, str_dev), jnp.int32),
            pltpu.VMEM((1, CB), jnp.int32),
            pltpu.SemaphoreType.DMA((6,)),
        ],
        hbm=[
            tokens,
            attention_gain[None],
            sequence_speaker_label[None],
            lengths[None],
            closing_gain[None],
            delays[None],
        ],
    )
    came = [swap(payload, "adapter", k) for k, payload in zip(peers, outgoing)]
    question_down, content_down = call(
        fetch_kernel,
        [pltpu.VMEM((voices * rank, d_slice), bf16)] * 2,
        [],
        scratch=[pltpu.SemaphoreType.DMA((8,))],
        hbm=[
            speaker_question_lowering.transpose(1, 2, 0).reshape(voices * rank, d_slice),
            speaker_content_lowering.transpose(1, 2, 0).reshape(voices * rank, d_slice),
        ],
        anywhere=[own_cols],
    )
    came, question_down = lax.optimization_barrier((came, question_down))
    other = swap(jnp.concatenate([piece[:half, :d_slice] for piece in came]), "tensor", 1)

    down, onehot = call(
        functools.partial(lowering_kernel, voices, rank),
        [shaped((n_adapter * slot_cap, 2 * rank), jnp.float32), shaped((n_adapter * slot_cap, 128), bf16)],
        [own_rows, *came],
        resident=[question_down, content_down],
    )
    other, down = lax.optimization_barrier((other, down))
    kept, sent = call(
        base_kernel,
        [shaped((2 * str_dev, query_columns + 2 * key_value_columns), jnp.float32)] * 2,
        [own_cols, *came, other],
        [place_ids],
        [pltpu.VMEM((n_adapter * str_dev, d_slice), bf16)],
        resident=[query_weight, key_weight, value_weight],
    )
    down = down + swap(down, "tensor", 1)
    summed = kept + swap(sent, "adapter", 1)
    raised = call(
        functools.partial(raising_kernel, voices, rank),
        [shaped((slot_cap, query_columns + key_value_columns), bf16)] * n_adapter,
        [down, swap(down, "tensor", 2), onehot],
        resident=[
            speaker_question_raising.reshape(voices * rank, query_columns),
            speaker_content_raising.reshape(voices * rank, key_value_columns),
        ],
    )
    returned = jnp.concatenate(
        [raised[0]] + [swap(raised[k], "adapter", k) for k in peers], axis=0
    )
    adapter_summands = jnp.einsum(
        "ms,mc->sc", placing, returned, preferred_element_type=jnp.float32
    )

    far = swap(summed[str_dev:], "adapter", 2)
    projected = summed[:str_dev] + far
    kv_local, ctx_len, head_dim = rotated_key_cache.shape[1:]
    group_size = query_columns // (kv_local * head_dim)
    query = rotate(
        (projected[:, :query_columns] + adapter_summands[:, :query_columns]).reshape(
            str_dev, kv_local, group_size, head_dim
        ),
        lengths,
    ).astype(jnp.bfloat16)
    key_base = projected[:, query_columns : query_columns + key_value_columns]
    key_new = rotate(key_base.reshape(str_dev, kv_local, head_dim), lengths).astype(jnp.bfloat16)
    value_new = (
        (projected[:, query_columns + key_value_columns :] + adapter_summands[:, query_columns:])
        .reshape(str_dev, kv_local, head_dim)
        .astype(jnp.bfloat16)
    )
    scale_factor = 1.0 / head_dim**0.5
    scores = (
        jnp.einsum("skgd,skcd->skgc", query, rotated_key_cache, preferred_element_type=jnp.float32)
        * scale_factor
    )
    own_score = (
        jnp.einsum("skgd,skd->skg", query, key_new, preferred_element_type=jnp.float32)
        * scale_factor
    )
    valid = (jnp.arange(ctx_len)[None, :] < lengths[:, None])[:, None, None, :]
    masked = jnp.where(valid, scores, -1e30)
    top_score = jnp.maximum(jnp.max(masked, axis=-1), own_score)
    weights_all = jnp.where(valid, jnp.exp(scores - top_score[..., None]), 0.0)
    own_weight = jnp.exp(own_score - top_score)
    total = jnp.sum(weights_all, axis=-1) + own_weight
    probs = (weights_all / total[..., None]).astype(jnp.bfloat16)
    own_prob = (own_weight / total).astype(jnp.bfloat16)
    mixed = jnp.einsum(
        "skgc,skcd->skgd", probs, stored_value_cache, preferred_element_type=jnp.float32
    )
    mixed = (
        mixed
        + own_prob.astype(jnp.float32)[..., None] * value_new.astype(jnp.float32)[:, :, None, :]
    )
    attended = mixed.astype(jnp.bfloat16).reshape(str_dev, query_columns)

    def with_raw(k):
        return jnp.concatenate([attended, raw[k]], axis=1)

    kept, sent = call(
        out_kernel,
        [shaped((2 * str_dev, d_slice), jnp.float32)] * 2,
        [with_raw(0)] + [swap(with_raw(k), "adapter", k) for k in peers],
        [place_ids],
        [pltpu.VMEM((n_adapter * str_dev, query_columns + quarter), bf16)],
        resident=[output_weight],
    )
    pair = kept + swap(sent, "tensor", 1)
    leaving = pair[str_dev:]
    largest = jnp.max(jnp.abs(leaving), axis=1, keepdims=True)
    row_scale = jnp.minimum(16384.0 / jnp.maximum(largest, 1e-30), 32768.0).astype(jnp.float16)
    coded = (leaving * row_scale.astype(jnp.float32)).astype(jnp.float16)
    coded = jnp.concatenate([coded, jnp.broadcast_to(row_scale, (str_dev, 128))], axis=1)
    coded = swap(coded, "tensor", 2)
    arrived = coded[:, :d_slice].astype(jnp.float32) / coded[:, d_slice : d_slice + 1].astype(jnp.float32)
    summed_out = pair[:str_dev] + arrived
    hidden_out = summed_out.astype(jnp.bfloat16)

    hidden_f = hidden_out.astype(jnp.float32)
    square = jnp.sum(hidden_f * hidden_f, axis=-1)
    square_sum = square
    for k in peers:
        square_sum = square_sum + swap(square, "adapter", k)
    scale = lax.rsqrt(square_sum / model_width + NORM_EPS)[None]
    across = swap(hidden_out, "tensor", 2)
    hidden_pair = swap(jnp.concatenate([hidden_out, across]), "tensor", 1)
    scale = jnp.concatenate([scale, swap(scale, "tensor", 2)])
    scale = jnp.concatenate([scale, swap(scale, "tensor", 1)])

    width = codebook_weight.shape[1] // 2
    outs = []

    def head(first, ids):
        return call(
            functools.partial(head_kernel, first),
            [shaped((2 * str_dev, width), jnp.float32)] * 2,
            [hidden_out, across, hidden_pair, scale, final_slice],
            [ids],
            [pltpu.VMEM((n_adapter * str_dev, d_slice), bf16)],
            resident=[codebook_weight],
        )

    def moved(block, k):
        return swap(block.astype(jnp.float16), "adapter", k).astype(jnp.float32)

    kept, sent = head(0, place_ids)
    kept, place_ids = lax.optimization_barrier((kept, place_ids))
    kept_far, sent_far = head(width, place_ids)
    kept = kept + moved(sent, 1)
    first_total = kept[:str_dev] + moved(kept[str_dev:], 2)
    second_total = (
        kept_far[:str_dev]
        + moved(sent_far[:str_dev], 1)
        + moved(kept_far[str_dev:], 2)
        + moved(sent_far[str_dev:], 3)
    )
    outs = [first_total * (1.0 / 16.0), second_total * (1.0 / 16.0)]
    if width == VOC:
        logits = jnp.stack([out * active[:, p : p + 1] for p, out in enumerate(outs)], axis=1)
    else:
        logits = jnp.concatenate(outs, axis=1).reshape(str_dev, books_local, VOC)
        logits = logits * active[:, :books_local, None]
    return (hidden_out, logits)


def per_device(
    tokens,
    attention_gain,
    query_weight,
    key_weight,
    value_weight,
    speaker_question_lowering,
    speaker_question_raising,
    speaker_content_lowering,
    speaker_content_raising,
    rotated_key_cache,
    stored_value_cache,
    sequence_speaker_label,
    lengths,
    output_weight,
    closing_gain,
    codebook_weight,
    delays,
):
    n_adapter = lax.axis_size("adapter")
    n_tensor = lax.axis_size("tensor")
    adapter_pos = lax.axis_index("adapter")
    tensor_pos = lax.axis_index("tensor")
    str_dev, model_width = tokens.shape
    all_streams = str_dev * n_adapter
    d_slice = model_width // n_adapter
    tensor_width = model_width // n_tensor
    tok_f = tokens.astype(jnp.float32)
    inverse = lax.rsqrt(jnp.mean(tok_f * tok_f, axis=-1, keepdims=True) + NORM_EPS)
    rescaled_hidden_state = (tok_f * inverse * attention_gain).astype(jnp.bfloat16)
    raw_cols, norm_cols = (
        lax.all_to_all(tokens, "adapter", split_axis=1, concat_axis=0, tiled=True),
        lax.all_to_all(rescaled_hidden_state, "adapter", split_axis=1, concat_axis=0, tiled=True),
    )
    query_columns = query_weight.shape[1]
    key_value_columns = key_weight.shape[1]
    weights_cat = jnp.concatenate([query_weight, key_weight, value_weight], axis=1)
    full_proj = jnp.dot(norm_cols, weights_cat, preferred_element_type=jnp.float32)
    summed = lax.psum(full_proj, "adapter")
    projected = lax.dynamic_slice_in_dim(summed, adapter_pos * str_dev, str_dev, 0)
    plain_query = projected[:, :query_columns]
    key_base = projected[:, query_columns : query_columns + key_value_columns]
    plain_value = projected[:, query_columns + key_value_columns :]
    voices_per_shard = speaker_question_raising.shape[0]
    adapter_rank_size = speaker_question_raising.shape[1]
    slot_cap = max(2, 2 * str_dev // n_adapter)
    slot_total = n_adapter * slot_cap
    owner_ids = sequence_speaker_label // voices_per_shard
    local_voice = sequence_speaker_label % voices_per_shard
    same_owner = owner_ids[:, None] == owner_ids[None, :]
    earlier = jnp.arange(str_dev)[:, None] > jnp.arange(str_dev)[None, :]
    owner_rank = jnp.sum((same_owner & earlier).astype(jnp.int32), axis=1)
    slot_ids = owner_ids * slot_cap + owner_rank
    placing = (slot_ids[None, :] == jnp.arange(slot_total)[:, None]).astype(jnp.bfloat16)
    voice_onehot = (local_voice[:, None] == jnp.arange(voices_per_shard)[None, :]).astype(
        jnp.bfloat16
    )
    normed_part = lax.dynamic_slice_in_dim(
        rescaled_hidden_state, tensor_pos * tensor_width, tensor_width, 1
    )
    send_rows = jnp.dot(placing, normed_part, preferred_element_type=jnp.float32).astype(
        jnp.bfloat16
    )
    send_voice = jnp.dot(placing, voice_onehot, preferred_element_type=jnp.float32).astype(
        jnp.bfloat16
    )
    send_rows = send_rows.reshape(n_adapter, slot_cap, tensor_width)
    send_voice = send_voice.reshape(n_adapter, slot_cap, voices_per_shard)
    query_down_matrix = speaker_question_lowering.reshape(
        tensor_width, voices_per_shard * adapter_rank_size
    )
    value_down_matrix = speaker_content_lowering.reshape(
        tensor_width, voices_per_shard * adapter_rank_size
    )
    query_up_matrix = speaker_question_raising.reshape(
        voices_per_shard * adapter_rank_size, query_columns
    )
    value_up_matrix = speaker_content_raising.reshape(
        voices_per_shard * adapter_rank_size, key_value_columns
    )
    rows_in = lax.all_to_all(send_rows, "adapter", split_axis=0, concat_axis=0, tiled=True)
    voices_in = lax.all_to_all(send_voice, "adapter", split_axis=0, concat_axis=0, tiled=True)
    item_count = rows_in.shape[1]
    flat_rows = rows_in.reshape(-1, tensor_width)
    onehot_b = voices_in.reshape(-1, voices_per_shard)
    onehot_f = onehot_b.astype(jnp.float32)
    all_q = jnp.dot(flat_rows, query_down_matrix, preferred_element_type=jnp.float32).reshape(
        -1, voices_per_shard, adapter_rank_size
    )
    all_v = jnp.dot(flat_rows, value_down_matrix, preferred_element_type=jnp.float32).reshape(
        -1, voices_per_shard, adapter_rank_size
    )
    down_q = jnp.sum(onehot_f[:, :, None] * all_q, axis=1)
    down_v = jnp.sum(onehot_f[:, :, None] * all_v, axis=1)
    down_q, down_v = lax.psum((down_q, down_v), "tensor")
    query_broadcast = (onehot_b[:, :, None] * down_q.astype(jnp.bfloat16)[:, None, :]).reshape(
        -1, voices_per_shard * adapter_rank_size
    )
    value_broadcast = (onehot_b[:, :, None] * down_v.astype(jnp.bfloat16)[:, None, :]).reshape(
        -1, voices_per_shard * adapter_rank_size
    )
    question_raised_product = (
        jnp.dot(query_broadcast, query_up_matrix, preferred_element_type=jnp.float32)
        * ADAPTER_SCALE
    ).astype(jnp.bfloat16)
    content_raised_product = (
        jnp.dot(value_broadcast, value_up_matrix, preferred_element_type=jnp.float32)
        * ADAPTER_SCALE
    ).astype(jnp.bfloat16)
    outgoing = jnp.concatenate([question_raised_product, content_raised_product], axis=1).reshape(
        n_adapter, item_count, query_columns + key_value_columns
    )
    returned = lax.all_to_all(outgoing, "adapter", split_axis=0, concat_axis=0, tiled=True)
    adapter_summands = jnp.einsum(
        "ms,mc->sc",
        placing,
        returned.reshape(slot_total, query_columns + key_value_columns),
        preferred_element_type=jnp.float32,
    )
    kv_local = rotated_key_cache.shape[1]
    head_dim = rotated_key_cache.shape[3]
    ctx_len = rotated_key_cache.shape[2]
    group_size = query_columns // (kv_local * head_dim)
    adapted_query = (plain_query + adapter_summands[:, :query_columns]).reshape(
        str_dev, kv_local, group_size, head_dim
    )
    query = rotate(adapted_query, lengths).astype(jnp.bfloat16)
    key_new = rotate(key_base.reshape(str_dev, kv_local, head_dim), lengths).astype(jnp.bfloat16)
    value_new = (
        (plain_value + adapter_summands[:, query_columns:])
        .reshape(str_dev, kv_local, head_dim)
        .astype(jnp.bfloat16)
    )
    scale_factor = 1.0 / head_dim**0.5
    scores = (
        jnp.einsum("skgd,skcd->skgc", query, rotated_key_cache, preferred_element_type=jnp.float32)
        * scale_factor
    )
    own_score = (
        jnp.einsum("skgd,skd->skg", query, key_new, preferred_element_type=jnp.float32)
        * scale_factor
    )
    valid = (jnp.arange(ctx_len)[None, :] < lengths[:, None])[:, None, None, :]
    masked = jnp.where(valid, scores, -1e30)
    top_score = jnp.maximum(jnp.max(masked, axis=-1), own_score)
    weights_all = jnp.where(valid, jnp.exp(scores - top_score[..., None]), 0.0)
    own_weight = jnp.exp(own_score - top_score)
    total = jnp.sum(weights_all, axis=-1) + own_weight
    probs = (weights_all / total[..., None]).astype(jnp.bfloat16)
    own_prob = (own_weight / total).astype(jnp.bfloat16)
    mixed = jnp.einsum(
        "skgc,skcd->skgd", probs, stored_value_cache, preferred_element_type=jnp.float32
    )
    mixed = (
        mixed
        + own_prob.astype(jnp.float32)[..., None] * value_new.astype(jnp.float32)[:, :, None, :]
    )
    attended = mixed.astype(jnp.bfloat16).reshape(str_dev, query_columns)
    partial_out = jnp.dot(
        lax.all_gather(attended, "adapter", axis=0, tiled=True),
        output_weight,
        preferred_element_type=jnp.float32,
    )
    final_slice = lax.dynamic_slice_in_dim(closing_gain, adapter_pos * d_slice, d_slice)
    rows_tensor = all_streams // n_tensor
    summed_out = lax.psum(partial_out, "tensor")
    hidden_all = (raw_cols.astype(jnp.float32) + summed_out).astype(jnp.bfloat16)
    hidden_f = hidden_all.astype(jnp.float32)
    square_sum = lax.psum(jnp.sum(hidden_f * hidden_f, axis=-1), "adapter")
    final_normed = (
        hidden_f * lax.rsqrt(square_sum / model_width + NORM_EPS)[:, None] * final_slice
    ).astype(jnp.bfloat16)
    hidden_out = lax.dynamic_slice_in_dim(hidden_all, tensor_pos * rows_tensor, rows_tensor, 0)
    logit_rows = lax.psum_scatter(
        jnp.dot(final_normed, codebook_weight, preferred_element_type=jnp.float32),
        "adapter",
        scatter_dimension=0,
        tiled=True,
    )
    books_local = CB // n_tensor
    book_delays = lax.dynamic_slice_in_dim(delays, tensor_pos * books_local, books_local)
    active = (lengths[:, None] >= book_delays[None, :]).astype(jnp.float32)
    logits = logit_rows.reshape(str_dev, books_local, VOC) * active[:, :, None]
    return (hidden_out, logits)


def solution(mesh):
    in_specs = (
        P(("groups", "adapter"), None),
        P(),
        P("adapter", "tensor"),
        P("adapter", "tensor"),
        P("adapter", "tensor"),
        P("tensor", "adapter", None),
        P("adapter", None, "tensor"),
        P("tensor", "adapter", None),
        P("adapter", None, "tensor"),
        P(("groups", "adapter"), "tensor", None, None),
        P(("groups", "adapter"), "tensor", None, None),
        P(("groups", "adapter")),
        P(("groups", "adapter")),
        P("tensor", "adapter"),
        P(),
        P("adapter", "tensor"),
        P(),
    )
    out_specs = (P(("groups", "tensor"), "adapter"), P(("groups", "adapter"), "tensor", None))
    four = mesh.shape["adapter"] == 4 and mesh.shape["tensor"] == 4
    return jax.shard_map(
        per_device_four if four else per_device, mesh=mesh, in_specs=in_specs, out_specs=out_specs, check_vma=False
    )
```

```python
import functools

import jax
import jax.numpy as jnp
from jax import lax
from jax.experimental import pallas as pl
from jax.experimental.pallas import tpu as pltpu
from jax.sharding import PartitionSpec as P

CB = 8
VOC = 2048


ROPE_BASE = 500000.0
NORM_EPS = 1e-05
ADAPTER_SCALE = 0.5
KERNEL_VMEM = 8 << 20


def rotate(values, positions):
    head_dim = values.shape[-1]
    half_dim = head_dim // 2
    spacing = jnp.arange(half_dim, dtype=jnp.float32) * (2.0 / head_dim)
    angles = positions.astype(jnp.float32)[:, None] * jnp.power(ROPE_BASE, -spacing)[None, :]
    new_shape = (values.shape[0],) + (1,) * (values.ndim - 2) + (half_dim,)
    cosine = jnp.cos(angles).reshape(new_shape)
    sine = jnp.sin(angles).reshape(new_shape)
    first_half = values[..., :half_dim]
    second_half = values[..., half_dim:]
    return jnp.concatenate(
        [first_half * cosine - second_half * sine, first_half * sine + second_half * cosine],
        axis=-1,
    )


def swap(value, axis, distance):
    size = lax.axis_size(axis)
    return lax.ppermute(value, axis, [(i, i ^ distance) for i in range(size)])


def take_block(array, index, size, axis=0):
    return lax.dynamic_slice_in_dim(array, index * size, size, axis)


def full_spec():
    return pl.BlockSpec(memory_space=pltpu.VMEM)


def call(kernel, outs, operands, scalars=(), scratch=(), resident=(), hbm=(), anywhere=()):
    hbm = [pltpu.with_memory_space_constraint(array, pltpu.HBM) for array in hbm]
    resident = [pltpu.with_memory_space_constraint(array, pltpu.VMEM) for array in resident]
    hbm += anywhere
    specs = [pl.BlockSpec(memory_space=pl.ANY)] * len(hbm)
    specs += [full_spec()] * (len(operands) + len(resident))
    arrays = [*hbm, *operands, *resident]
    specs = [pl.BlockSpec(memory_space=pltpu.SMEM)] * len(scalars) + specs
    arrays = [*scalars, *arrays]
    return pl.pallas_call(
        kernel,
        out_shape=tuple(outs),
        in_specs=specs,
        out_specs=tuple(full_spec() for _ in outs),
        scratch_shapes=scratch,
        cost_estimate=pl.CostEstimate(flops=1000, bytes_accessed=1000, transcendentals=0),
        compiler_params=pltpu.CompilerParams(vmem_limit_bytes=KERNEL_VMEM),
    )(*arrays)


def shaped(shape, dtype):
    return jax.ShapeDtypeStruct(shape, dtype)


def norm_kernel(
    n_adapter, voices, books, place_ref,
    tokens_hbm, gain_hbm, label_hbm, lengths_hbm, closing_hbm, delays_hbm,
    own_ref, rows_ref, out1_ref, out2_ref, out3_ref, placing_ref, raw_ref, active_ref, closing_ref,
    normed_ref, tokens_ref, gain_ref, label_ref, lengths_ref, delays_ref, sems,
):
    a, t = place_ref[0], place_ref[1]
    streams, model_width = tokens_ref.shape
    d_slice = own_ref.shape[1]
    closing_part = closing_hbm.at[:, pl.ds(pl.multiple_of(a * d_slice, d_slice), d_slice)]
    copies = [
        pltpu.make_async_copy(source, target, sems.at[i])
        for i, (source, target) in enumerate(
            (
                (tokens_hbm, tokens_ref),
                (gain_hbm, gain_ref),
                (label_hbm, label_ref),
                (lengths_hbm, lengths_ref),
                (closing_part, closing_ref),
                (delays_hbm, delays_ref),
            )
        )
    ]
    for copy in copies:
        copy.start()
    for copy in copies:
        copy.wait()
    half = streams // 2
    cap = rows_ref.shape[0]
    tok = tokens_ref[...].astype(jnp.float32)
    mean = jnp.sum(tok * tok, axis=-1, keepdims=True) * (1.0 / model_width)
    normed_ref[...] = (tok * lax.rsqrt(mean + NORM_EPS) * gain_ref[...]).astype(jnp.bfloat16)

    def owner_of(label):
        return sum((label >= j * voices).astype(jnp.int32) for j in range(1, n_adapter))

    square = (streams, streams)
    row_index = lax.broadcasted_iota(jnp.int32, square, 0)
    col_index = lax.broadcasted_iota(jnp.int32, square, 1)

    def column(row):
        picked = jnp.where(row_index == col_index, row.astype(jnp.float32), 0.0)
        return jnp.sum(picked, axis=1, keepdims=True).astype(jnp.int32)

    label_row = label_ref[...]
    label_col = column(label_row)
    owner_row, owner_col = owner_of(label_row), owner_of(label_col)
    voice = label_col - owner_col * voices
    earlier = (owner_col == owner_row) & (row_index < col_index)
    rank = jnp.sum(earlier.astype(jnp.float32), axis=0, keepdims=True).astype(jnp.int32)
    slot = jnp.bitwise_xor(owner_row, a) * cap + rank
    slots = (n_adapter * cap, streams)
    placing = (lax.broadcasted_iota(jnp.int32, slots, 0) == slot).astype(jnp.float32).astype(jnp.bfloat16)
    placing_ref[...] = placing
    lanes = (streams, 128)
    onehot = (lax.broadcasted_iota(jnp.int32, lanes, 1) == voice).astype(jnp.float32).astype(jnp.bfloat16)
    mine = normed_ref[:, pl.ds(pl.multiple_of(t * d_slice, d_slice), d_slice)]
    rows = jnp.dot(placing, mine, preferred_element_type=jnp.float32).astype(jnp.bfloat16)
    kinds = jnp.dot(placing, onehot, preferred_element_type=jnp.float32).astype(jnp.bfloat16)
    own_ref[...] = normed_ref[:, pl.ds(pl.multiple_of(a * d_slice, d_slice), d_slice)]
    rows_ref[:, :d_slice] = rows[:cap]
    rows_ref[:, d_slice:] = kinds[:cap]
    first = pl.multiple_of(lax.rem(t, 2) * half, half)
    length_col = column(lengths_ref[...])
    lane = lax.broadcasted_iota(jnp.int32, active_ref.shape, 1)
    active = jnp.zeros(active_ref.shape, jnp.float32)
    books_row = delays_ref[...].astype(jnp.float32)
    book = lax.broadcasted_iota(jnp.int32, books_row.shape, 1)
    for p in range(books):
        mine_only = jnp.where(book == t * books + p, books_row, 0.0)
        delay = jnp.sum(mine_only, axis=1, keepdims=True).astype(jnp.int32)
        started = (length_col >= delay).astype(jnp.float32)
        active = jnp.where(lane == p, started, active)
    active_ref[...] = active
    quarter = raw_ref.shape[2]
    for k in range(n_adapter):
        first_raw = pl.multiple_of(jnp.bitwise_xor(a, k) * d_slice + t * quarter, quarter)
        raw_ref[k] = tokens_ref[:, pl.ds(first_raw, quarter)]
    for k, out_ref in enumerate((out1_ref, out2_ref, out3_ref), 1):
        start = pl.multiple_of(jnp.bitwise_xor(a, k) * d_slice, d_slice)
        out_ref[:half, :d_slice] = normed_ref[pl.ds(first, half), pl.ds(start, d_slice)]
        out_ref[:half, d_slice:] = jnp.zeros((half, 128), jnp.bfloat16)
        out_ref[half:, :d_slice] = rows[k * cap : (k + 1) * cap]
        out_ref[half:, d_slice:] = kinds[k * cap : (k + 1) * cap]


def fetch_kernel(question_hbm, content_hbm, after_hbm, question_ref, content_ref, sems):
    copies = []
    for source, target in ((question_hbm, question_ref), (content_hbm, content_ref)):
        rows = source.shape[0] // 4
        for i in range(4):
            part = pl.ds(i * rows, rows)
            copies.append(
                pltpu.make_async_copy(source.at[part], target.at[part], sems.at[len(copies)])
            )
    for copy in copies:
        copy.start()
    for copy in copies:
        copy.wait()


def lowering_kernel(
    voices, rank, own_ref, in1_ref, in2_ref, in3_ref, question_ref, content_ref, down_ref, onehot_ref
):
    width = question_ref.shape[1]
    cap = own_ref.shape[0]
    rows = jnp.concatenate(
        [own_ref[...], in1_ref[cap:, :], in2_ref[cap:, :], in3_ref[cap:, :]], axis=0
    )
    onehot = rows[:, width:]
    onehot_ref[...] = onehot
    onehot = onehot.astype(jnp.float32)
    left = lax.broadcasted_iota(jnp.int32, (rows.shape[0], 2 * rank), 1) < rank
    sums = []
    for weight_ref in (question_ref, content_ref):
        every = lax.dot_general(
            rows[:, :width],
            weight_ref[...],
            (((1,), (1,)), ((), ())),
            preferred_element_type=jnp.float32,
        )
        kept = 0.0
        for pair in range(voices // 2):
            mask = jnp.where(left, onehot[:, 2 * pair : 2 * pair + 1], onehot[:, 2 * pair + 1 : 2 * pair + 2])
            kept = kept + mask * every[:, 2 * pair * rank : 2 * (pair + 1) * rank]
        sums.append(kept[:, :rank] + kept[:, rank:])
    down_ref[...] = jnp.concatenate(sums, axis=1)


def raising_kernel(
    voices, rank, near_ref, far_ref, onehot_ref, question_ref, content_ref,
    own_ref, out1_ref, out2_ref, out3_ref,
):
    down = (near_ref[...] + far_ref[...]).astype(jnp.bfloat16).astype(jnp.float32)
    onehot = onehot_ref[...].astype(jnp.float32)
    left = lax.broadcasted_iota(jnp.int32, (down.shape[0], 2 * rank), 1) < rank
    first = 0
    for i, weight_ref in enumerate((question_ref, content_ref)):
        part = down[:, i * rank : (i + 1) * rank]
        twice = jnp.concatenate([part, part], axis=1)
        spread = jnp.concatenate(
            [
                jnp.where(left, onehot[:, 2 * pair : 2 * pair + 1], onehot[:, 2 * pair + 1 : 2 * pair + 2])
                * twice
                for pair in range(voices // 2)
            ],
            axis=1,
        ).astype(jnp.bfloat16)
        up = jnp.dot(spread, weight_ref[...], preferred_element_type=jnp.float32) * ADAPTER_SCALE
        up = up.astype(jnp.bfloat16)
        last = first + weight_ref.shape[1]
        cap = own_ref.shape[0]
        for k, out_ref in enumerate((own_ref, out1_ref, out2_ref, out3_ref)):
            out_ref[:, first:last] = up[k * cap : (k + 1) * cap]
        first = last


def base_kernel(
    place_ref, own_ref, in1_ref, in2_ref, in3_ref, other_ref, query_ref, key_ref, value_ref,
    keep_ref, send_ref, rows_ref,
):
    core = lax.rem(place_ref[1], 2)
    streams, width = own_ref.shape
    half = streams // 2
    rows_ref[:streams, :] = own_ref[...]
    for k, in_ref in enumerate((in1_ref, in2_ref, in3_ref), 1):
        mine = pl.multiple_of(k * streams + core * half, half)
        theirs = pl.multiple_of(k * streams + (1 - core) * half, half)
        rows_ref[pl.ds(mine, half), :] = in_ref[:half, :width]
        rows_ref[pl.ds(theirs, half), :] = other_ref[(k - 1) * half : k * half, :]
    first = 0
    for weight_ref in (query_ref, key_ref, value_ref):
        last = first + weight_ref.shape[1]
        out = jnp.dot(rows_ref[...], weight_ref[...], preferred_element_type=jnp.float32)
        for k in range(4):
            out_ref = send_ref if k % 2 else keep_ref
            out_ref[k // 2 * streams : (k // 2 + 1) * streams, first:last] = out[
                k * streams : (k + 1) * streams
            ]
        first = last


def out_kernel(
    place_ref, own_ref, in1_ref, in2_ref, in3_ref, weight_ref, keep_ref, send_ref, rows_ref
):
    turn = jnp.bitwise_xor(place_ref[0], place_ref[1])
    streams = own_ref.shape[0]
    for k, in_ref in enumerate((own_ref, in1_ref, in2_ref, in3_ref)):
        first = pl.multiple_of(jnp.bitwise_xor(turn, k) * streams, streams)
        rows_ref[pl.ds(first, streams), :] = in_ref[...]
    depth = weight_ref.shape[0]
    quarter = rows_ref.shape[1] - depth
    column = pl.ds(pl.multiple_of(place_ref[1] * quarter, quarter), quarter)
    out = jnp.dot(rows_ref[:, :depth], weight_ref[...], preferred_element_type=jnp.float32)
    for m in range(4):
        out_ref = send_ref if m % 2 else keep_ref
        to, block = pl.ds(m // 2 * streams, streams), slice(m * streams, (m + 1) * streams)
        out_ref[to, :] = out[block]
        out_ref[to, column] += rows_ref[block, depth:].astype(jnp.float32)


def head_kernel(
    first, place_ref, own_ref, across_ref, pair_ref, scale_ref, gain_ref, weight_ref, keep_ref, send_ref, rows_ref
):
    turn = jnp.bitwise_xor(place_ref[0], place_ref[1])
    streams = own_ref.shape[0]
    diagonal = lax.broadcasted_iota(jnp.int32, (streams, streams), 0) == lax.broadcasted_iota(
        jnp.int32, (streams, streams), 1
    )
    pieces = (
        own_ref[...],
        pair_ref[:streams, :],
        across_ref[...],
        pair_ref[streams:, :],
    )
    for m, piece in enumerate(pieces):
        row = (0, 2, 1, 3)[m]
        scale = jnp.sum(
            jnp.where(diagonal, scale_ref[row : row + 1, :], 0.0), axis=1, keepdims=True
        )
        at = pl.multiple_of(jnp.bitwise_xor(turn, m) * streams, streams)
        rows_ref[pl.ds(at, streams), :] = (
            piece.astype(jnp.float32) * scale * gain_ref[...]
        ).astype(jnp.bfloat16)
    width = keep_ref.shape[1]
    out = 16.0 * jnp.dot(
        rows_ref[...], weight_ref[:, first : first + width], preferred_element_type=jnp.float32
    )
    keep_ref[:streams] = out[:streams]
    send_ref[:streams] = out[streams : 2 * streams]
    keep_ref[streams:] = out[2 * streams : 3 * streams]
    send_ref[streams:] = out[3 * streams :]


LEVELS = 30719.0
LEVEL_STEP = 16416.0 / LEVELS


def row_root(values):
    largest = jnp.max(jnp.abs(values), axis=1, keepdims=True)
    root = jnp.sqrt(16384.0 / jnp.maximum(largest, 1e-30))
    return lax.reduce_precision(jnp.minimum(root, 65504.0), 5, 10)


def encode(values, root):
    scaled = values * (root * root) * (1.0 / LEVEL_STEP)
    place = (jnp.round(jnp.abs(scaled)) + 1024.0) * (1.0 / 1024.0)
    power = jnp.floor(place)
    size = (1.0 + (place - power)) * jnp.exp2(power - 15.0)
    code = jnp.where(scaled < 0, -size, size).astype(jnp.float16)
    root = jnp.broadcast_to(root.astype(jnp.float16), (values.shape[0], 128))
    return jnp.concatenate([code, root], axis=1)


def decode(coded, width):
    code = coded[:, :width].astype(jnp.float32)
    root = coded[:, width : width + 1].astype(jnp.float32)
    size = jnp.abs(code)
    power = jnp.floor(jnp.log2(size))
    steps = jnp.round((power + 14.0 + (size * jnp.exp2(-power) - 1.0)) * 1024.0)
    return jnp.where(code < 0, -steps, steps) * (LEVEL_STEP / (root * root))


def per_device_four(
    tokens,
    attention_gain,
    query_weight,
    key_weight,
    value_weight,
    speaker_question_lowering,
    speaker_question_raising,
    speaker_content_lowering,
    speaker_content_raising,
    rotated_key_cache,
    stored_value_cache,
    sequence_speaker_label,
    lengths,
    output_weight,
    closing_gain,
    codebook_weight,
    delays,
):
    n_adapter = lax.axis_size("adapter")
    peers = range(1, n_adapter)
    a = lax.axis_index("adapter")
    t = lax.axis_index("tensor")
    str_dev, model_width = tokens.shape
    place_ids = jnp.stack([a, t]).astype(jnp.int32)
    d_slice = model_width // n_adapter
    voices, rank = speaker_question_raising.shape[:2]
    query_columns = query_weight.shape[1]
    key_value_columns = key_weight.shape[1]

    bf16 = jnp.bfloat16
    slot_cap = max(2, 2 * str_dev // n_adapter)
    half = str_dev // 2
    n_tensor = lax.axis_size("tensor")
    quarter = d_slice // n_tensor
    books_local = CB // n_tensor
    own_cols, own_rows, *outgoing, placing, raw, active, final_slice = call(
        functools.partial(norm_kernel, n_adapter, voices, books_local),
        [shaped((str_dev, d_slice), bf16), shaped((slot_cap, d_slice + 128), bf16)]
        + [shaped((half + slot_cap, d_slice + 128), bf16)] * 3
        + [
            shaped((n_adapter * slot_cap, str_dev), bf16),
            shaped((n_adapter, str_dev, quarter), bf16),
            shaped((str_dev, 128), jnp.float32),
            shaped((1, d_slice), jnp.float32),
        ],
        [],
        [place_ids],
        [
            pltpu.VMEM((str_dev, model_width), bf16),
            pltpu.VMEM((str_dev, model_width), bf16),
            pltpu.VMEM((1, model_width), jnp.float32),
            pltpu.VMEM((1, str_dev), jnp.int32),
            pltpu.VMEM((1, str_dev), jnp.int32),
            pltpu.VMEM((1, CB), jnp.int32),
            pltpu.SemaphoreType.DMA((6,)),
        ],
        hbm=[
            tokens,
            attention_gain[None],
            sequence_speaker_label[None],
            lengths[None],
            closing_gain[None],
            delays[None],
        ],
    )
    came = [swap(payload, "adapter", k) for k, payload in zip(peers, outgoing)]
    question_down, content_down = call(
        fetch_kernel,
        [pltpu.VMEM((voices * rank, d_slice), bf16)] * 2,
        [],
        scratch=[pltpu.SemaphoreType.DMA((8,))],
        hbm=[
            speaker_question_lowering.transpose(1, 2, 0).reshape(voices * rank, d_slice),
            speaker_content_lowering.transpose(1, 2, 0).reshape(voices * rank, d_slice),
        ],
        anywhere=[own_cols],
    )
    came, question_down = lax.optimization_barrier((came, question_down))
    other = swap(jnp.concatenate([piece[:half, :d_slice] for piece in came]), "tensor", 1)

    down, onehot = call(
        functools.partial(lowering_kernel, voices, rank),
        [shaped((n_adapter * slot_cap, 2 * rank), jnp.float32), shaped((n_adapter * slot_cap, 128), bf16)],
        [own_rows, *came],
        resident=[question_down, content_down],
    )
    other, down = lax.optimization_barrier((other, down))
    kept, sent = call(
        base_kernel,
        [shaped((2 * str_dev, query_columns + 2 * key_value_columns), jnp.float32)] * 2,
        [own_cols, *came, other],
        [place_ids],
        [pltpu.VMEM((n_adapter * str_dev, d_slice), bf16)],
        resident=[query_weight, key_weight, value_weight],
    )
    down = down + swap(down, "tensor", 1)
    summed = kept + swap(sent, "adapter", 1)
    raised = call(
        functools.partial(raising_kernel, voices, rank),
        [shaped((slot_cap, query_columns + key_value_columns), bf16)] * n_adapter,
        [down, swap(down, "tensor", 2), onehot],
        resident=[
            speaker_question_raising.reshape(voices * rank, query_columns),
            speaker_content_raising.reshape(voices * rank, key_value_columns),
        ],
    )
    returned = jnp.concatenate(
        [raised[0]] + [swap(raised[k], "adapter", k) for k in peers], axis=0
    )
    adapter_summands = jnp.einsum(
        "ms,mc->sc", placing, returned, preferred_element_type=jnp.float32
    )

    far = swap(summed[str_dev:], "adapter", 2)
    projected = summed[:str_dev] + far
    kv_local, ctx_len, head_dim = rotated_key_cache.shape[1:]
    group_size = query_columns // (kv_local * head_dim)
    query = rotate(
        (projected[:, :query_columns] + adapter_summands[:, :query_columns]).reshape(
            str_dev, kv_local, group_size, head_dim
        ),
        lengths,
    ).astype(jnp.bfloat16)
    key_base = projected[:, query_columns : query_columns + key_value_columns]
    key_new = rotate(key_base.reshape(str_dev, kv_local, head_dim), lengths).astype(jnp.bfloat16)
    value_new = (
        (projected[:, query_columns + key_value_columns :] + adapter_summands[:, query_columns:])
        .reshape(str_dev, kv_local, head_dim)
        .astype(jnp.bfloat16)
    )
    scale_factor = 1.0 / head_dim**0.5
    scores = (
        jnp.einsum("skgd,skcd->skgc", query, rotated_key_cache, preferred_element_type=jnp.float32)
        * scale_factor
    )
    own_score = (
        jnp.einsum("skgd,skd->skg", query, key_new, preferred_element_type=jnp.float32)
        * scale_factor
    )
    valid = (jnp.arange(ctx_len)[None, :] < lengths[:, None])[:, None, None, :]
    masked = jnp.where(valid, scores, -1e30)
    top_score = jnp.maximum(jnp.max(masked, axis=-1), own_score)
    weights_all = jnp.where(valid, jnp.exp(scores - top_score[..., None]), 0.0)
    own_weight = jnp.exp(own_score - top_score)
    total = jnp.sum(weights_all, axis=-1) + own_weight
    probs = (weights_all / total[..., None]).astype(jnp.bfloat16)
    own_prob = (own_weight / total).astype(jnp.bfloat16)
    mixed = jnp.einsum(
        "skgc,skcd->skgd", probs, stored_value_cache, preferred_element_type=jnp.float32
    )
    mixed = (
        mixed
        + own_prob.astype(jnp.float32)[..., None] * value_new.astype(jnp.float32)[:, :, None, :]
    )
    attended = mixed.astype(jnp.bfloat16).reshape(str_dev, query_columns)

    def with_raw(k):
        return jnp.concatenate([attended, raw[k]], axis=1)

    kept, sent = call(
        out_kernel,
        [shaped((2 * str_dev, d_slice), jnp.float32)] * 2,
        [with_raw(0)] + [swap(with_raw(k), "adapter", k) for k in peers],
        [place_ids],
        [pltpu.VMEM((n_adapter * str_dev, query_columns + quarter), bf16)],
        resident=[output_weight],
    )
    pair = kept + swap(sent, "tensor", 1)
    pair_scale = row_root(pair[str_dev:])
    coded = swap(encode(pair[str_dev:], pair_scale), "tensor", 2)
    arrived = decode(coded, d_slice)
    summed_out = pair[:str_dev] + arrived
    hidden_out = summed_out.astype(jnp.bfloat16)

    hidden_f = hidden_out.astype(jnp.float32)
    square = jnp.sum(hidden_f * hidden_f, axis=-1)
    square_sum = square
    for k in peers:
        square_sum = square_sum + swap(square, "adapter", k)
    scale = lax.rsqrt(square_sum / model_width + NORM_EPS)[None]
    across = swap(hidden_out, "tensor", 2)
    hidden_pair = swap(jnp.concatenate([hidden_out, across]), "tensor", 1)
    scale = jnp.concatenate([scale, swap(scale, "tensor", 2)])
    scale = jnp.concatenate([scale, swap(scale, "tensor", 1)])

    width = codebook_weight.shape[1] // 2
    outs = []

    def head(first, ids):
        return call(
            functools.partial(head_kernel, first),
            [shaped((2 * str_dev, width), jnp.float32)] * 2,
            [hidden_out, across, hidden_pair, scale, final_slice],
            [ids],
            [pltpu.VMEM((n_adapter * str_dev, d_slice), bf16)],
            resident=[codebook_weight],
        )

    def moved(block, k):
        return swap(block.astype(jnp.float16), "adapter", k).astype(jnp.float32)

    kept, sent = head(0, place_ids)
    kept, place_ids = lax.optimization_barrier((kept, place_ids))
    kept_far, sent_far = head(width, place_ids)
    kept = kept + moved(sent, 1)
    first_total = kept[:str_dev] + moved(kept[str_dev:], 2)
    second_total = (
        kept_far[:str_dev]
        + moved(sent_far[:str_dev], 1)
        + moved(kept_far[str_dev:], 2)
        + moved(sent_far[str_dev:], 3)
    )
    outs = [first_total * (1.0 / 16.0), second_total * (1.0 / 16.0)]
    if width == VOC:
        logits = jnp.stack([out * active[:, p : p + 1] for p, out in enumerate(outs)], axis=1)
    else:
        logits = jnp.concatenate(outs, axis=1).reshape(str_dev, books_local, VOC)
        logits = logits * active[:, :books_local, None]
    return (hidden_out, logits)


def per_device(
    tokens,
    attention_gain,
    query_weight,
    key_weight,
    value_weight,
    speaker_question_lowering,
    speaker_question_raising,
    speaker_content_lowering,
    speaker_content_raising,
    rotated_key_cache,
    stored_value_cache,
    sequence_speaker_label,
    lengths,
    output_weight,
    closing_gain,
    codebook_weight,
    delays,
):
    n_adapter = lax.axis_size("adapter")
    n_tensor = lax.axis_size("tensor")
    adapter_pos = lax.axis_index("adapter")
    tensor_pos = lax.axis_index("tensor")
    str_dev, model_width = tokens.shape
    all_streams = str_dev * n_adapter
    d_slice = model_width // n_adapter
    tensor_width = model_width // n_tensor
    tok_f = tokens.astype(jnp.float32)
    inverse = lax.rsqrt(jnp.mean(tok_f * tok_f, axis=-1, keepdims=True) + NORM_EPS)
    rescaled_hidden_state = (tok_f * inverse * attention_gain).astype(jnp.bfloat16)
    raw_cols, norm_cols = (
        lax.all_to_all(tokens, "adapter", split_axis=1, concat_axis=0, tiled=True),
        lax.all_to_all(rescaled_hidden_state, "adapter", split_axis=1, concat_axis=0, tiled=True),
    )
    query_columns = query_weight.shape[1]
    key_value_columns = key_weight.shape[1]
    weights_cat = jnp.concatenate([query_weight, key_weight, value_weight], axis=1)
    full_proj = jnp.dot(norm_cols, weights_cat, preferred_element_type=jnp.float32)
    summed = lax.psum(full_proj, "adapter")
    projected = lax.dynamic_slice_in_dim(summed, adapter_pos * str_dev, str_dev, 0)
    plain_query = projected[:, :query_columns]
    key_base = projected[:, query_columns : query_columns + key_value_columns]
    plain_value = projected[:, query_columns + key_value_columns :]
    voices_per_shard = speaker_question_raising.shape[0]
    adapter_rank_size = speaker_question_raising.shape[1]
    slot_cap = max(2, 2 * str_dev // n_adapter)
    slot_total = n_adapter * slot_cap
    owner_ids = sequence_speaker_label // voices_per_shard
    local_voice = sequence_speaker_label % voices_per_shard
    same_owner = owner_ids[:, None] == owner_ids[None, :]
    earlier = jnp.arange(str_dev)[:, None] > jnp.arange(str_dev)[None, :]
    owner_rank = jnp.sum((same_owner & earlier).astype(jnp.int32), axis=1)
    slot_ids = owner_ids * slot_cap + owner_rank
    placing = (slot_ids[None, :] == jnp.arange(slot_total)[:, None]).astype(jnp.bfloat16)
    voice_onehot = (local_voice[:, None] == jnp.arange(voices_per_shard)[None, :]).astype(
        jnp.bfloat16
    )
    normed_part = lax.dynamic_slice_in_dim(
        rescaled_hidden_state, tensor_pos * tensor_width, tensor_width, 1
    )
    send_rows = jnp.dot(placing, normed_part, preferred_element_type=jnp.float32).astype(
        jnp.bfloat16
    )
    send_voice = jnp.dot(placing, voice_onehot, preferred_element_type=jnp.float32).astype(
        jnp.bfloat16
    )
    send_rows = send_rows.reshape(n_adapter, slot_cap, tensor_width)
    send_voice = send_voice.reshape(n_adapter, slot_cap, voices_per_shard)
    query_down_matrix = speaker_question_lowering.reshape(
        tensor_width, voices_per_shard * adapter_rank_size
    )
    value_down_matrix = speaker_content_lowering.reshape(
        tensor_width, voices_per_shard * adapter_rank_size
    )
    query_up_matrix = speaker_question_raising.reshape(
        voices_per_shard * adapter_rank_size, query_columns
    )
    value_up_matrix = speaker_content_raising.reshape(
        voices_per_shard * adapter_rank_size, key_value_columns
    )
    rows_in = lax.all_to_all(send_rows, "adapter", split_axis=0, concat_axis=0, tiled=True)
    voices_in = lax.all_to_all(send_voice, "adapter", split_axis=0, concat_axis=0, tiled=True)
    item_count = rows_in.shape[1]
    flat_rows = rows_in.reshape(-1, tensor_width)
    onehot_b = voices_in.reshape(-1, voices_per_shard)
    onehot_f = onehot_b.astype(jnp.float32)
    all_q = jnp.dot(flat_rows, query_down_matrix, preferred_element_type=jnp.float32).reshape(
        -1, voices_per_shard, adapter_rank_size
    )
    all_v = jnp.dot(flat_rows, value_down_matrix, preferred_element_type=jnp.float32).reshape(
        -1, voices_per_shard, adapter_rank_size
    )
    down_q = jnp.sum(onehot_f[:, :, None] * all_q, axis=1)
    down_v = jnp.sum(onehot_f[:, :, None] * all_v, axis=1)
    down_q, down_v = lax.psum((down_q, down_v), "tensor")
    query_broadcast = (onehot_b[:, :, None] * down_q.astype(jnp.bfloat16)[:, None, :]).reshape(
        -1, voices_per_shard * adapter_rank_size
    )
    value_broadcast = (onehot_b[:, :, None] * down_v.astype(jnp.bfloat16)[:, None, :]).reshape(
        -1, voices_per_shard * adapter_rank_size
    )
    question_raised_product = (
        jnp.dot(query_broadcast, query_up_matrix, preferred_element_type=jnp.float32)
        * ADAPTER_SCALE
    ).astype(jnp.bfloat16)
    content_raised_product = (
        jnp.dot(value_broadcast, value_up_matrix, preferred_element_type=jnp.float32)
        * ADAPTER_SCALE
    ).astype(jnp.bfloat16)
    outgoing = jnp.concatenate([question_raised_product, content_raised_product], axis=1).reshape(
        n_adapter, item_count, query_columns + key_value_columns
    )
    returned = lax.all_to_all(outgoing, "adapter", split_axis=0, concat_axis=0, tiled=True)
    adapter_summands = jnp.einsum(
        "ms,mc->sc",
        placing,
        returned.reshape(slot_total, query_columns + key_value_columns),
        preferred_element_type=jnp.float32,
    )
    kv_local = rotated_key_cache.shape[1]
    head_dim = rotated_key_cache.shape[3]
    ctx_len = rotated_key_cache.shape[2]
    group_size = query_columns // (kv_local * head_dim)
    adapted_query = (plain_query + adapter_summands[:, :query_columns]).reshape(
        str_dev, kv_local, group_size, head_dim
    )
    query = rotate(adapted_query, lengths).astype(jnp.bfloat16)
    key_new = rotate(key_base.reshape(str_dev, kv_local, head_dim), lengths).astype(jnp.bfloat16)
    value_new = (
        (plain_value + adapter_summands[:, query_columns:])
        .reshape(str_dev, kv_local, head_dim)
        .astype(jnp.bfloat16)
    )
    scale_factor = 1.0 / head_dim**0.5
    scores = (
        jnp.einsum("skgd,skcd->skgc", query, rotated_key_cache, preferred_element_type=jnp.float32)
        * scale_factor
    )
    own_score = (
        jnp.einsum("skgd,skd->skg", query, key_new, preferred_element_type=jnp.float32)
        * scale_factor
    )
    valid = (jnp.arange(ctx_len)[None, :] < lengths[:, None])[:, None, None, :]
    masked = jnp.where(valid, scores, -1e30)
    top_score = jnp.maximum(jnp.max(masked, axis=-1), own_score)
    weights_all = jnp.where(valid, jnp.exp(scores - top_score[..., None]), 0.0)
    own_weight = jnp.exp(own_score - top_score)
    total = jnp.sum(weights_all, axis=-1) + own_weight
    probs = (weights_all / total[..., None]).astype(jnp.bfloat16)
    own_prob = (own_weight / total).astype(jnp.bfloat16)
    mixed = jnp.einsum(
        "skgc,skcd->skgd", probs, stored_value_cache, preferred_element_type=jnp.float32
    )
    mixed = (
        mixed
        + own_prob.astype(jnp.float32)[..., None] * value_new.astype(jnp.float32)[:, :, None, :]
    )
    attended = mixed.astype(jnp.bfloat16).reshape(str_dev, query_columns)
    partial_out = jnp.dot(
        lax.all_gather(attended, "adapter", axis=0, tiled=True),
        output_weight,
        preferred_element_type=jnp.float32,
    )
    final_slice = lax.dynamic_slice_in_dim(closing_gain, adapter_pos * d_slice, d_slice)
    rows_tensor = all_streams // n_tensor
    summed_out = lax.psum(partial_out, "tensor")
    hidden_all = (raw_cols.astype(jnp.float32) + summed_out).astype(jnp.bfloat16)
    hidden_f = hidden_all.astype(jnp.float32)
    square_sum = lax.psum(jnp.sum(hidden_f * hidden_f, axis=-1), "adapter")
    final_normed = (
        hidden_f * lax.rsqrt(square_sum / model_width + NORM_EPS)[:, None] * final_slice
    ).astype(jnp.bfloat16)
    hidden_out = lax.dynamic_slice_in_dim(hidden_all, tensor_pos * rows_tensor, rows_tensor, 0)
    logit_rows = lax.psum_scatter(
        jnp.dot(final_normed, codebook_weight, preferred_element_type=jnp.float32),
        "adapter",
        scatter_dimension=0,
        tiled=True,
    )
    books_local = CB // n_tensor
    book_delays = lax.dynamic_slice_in_dim(delays, tensor_pos * books_local, books_local)
    active = (lengths[:, None] >= book_delays[None, :]).astype(jnp.float32)
    logits = logit_rows.reshape(str_dev, books_local, VOC) * active[:, :, None]
    return (hidden_out, logits)


def solution(mesh):
    in_specs = (
        P(("groups", "adapter"), None),
        P(),
        P("adapter", "tensor"),
        P("adapter", "tensor"),
        P("adapter", "tensor"),
        P("tensor", "adapter", None),
        P("adapter", None, "tensor"),
        P("tensor", "adapter", None),
        P("adapter", None, "tensor"),
        P(("groups", "adapter"), "tensor", None, None),
        P(("groups", "adapter"), "tensor", None, None),
        P(("groups", "adapter")),
        P(("groups", "adapter")),
        P("tensor", "adapter"),
        P(),
        P("adapter", "tensor"),
        P(),
    )
    out_specs = (P(("groups", "tensor"), "adapter"), P(("groups", "adapter"), "tensor", None))
    four = mesh.shape["adapter"] == 4 and mesh.shape["tensor"] == 4
    return jax.shard_map(
        per_device_four if four else per_device, mesh=mesh, in_specs=in_specs, out_specs=out_specs, check_vma=False
    )
```

```python
import functools

import jax
import jax.numpy as jnp
from jax import lax
from jax.experimental import pallas as pl
from jax.experimental.pallas import tpu as pltpu
from jax.sharding import PartitionSpec as P

CB = 8
VOC = 2048


ROPE_BASE = 500000.0
NORM_EPS = 1e-05
ADAPTER_SCALE = 0.5
KERNEL_VMEM = 8 << 20


def rotate(values, positions):
    head_dim = values.shape[-1]
    half_dim = head_dim // 2
    spacing = jnp.arange(half_dim, dtype=jnp.float32) * (2.0 / head_dim)
    angles = positions.astype(jnp.float32)[:, None] * jnp.power(ROPE_BASE, -spacing)[None, :]
    new_shape = (values.shape[0],) + (1,) * (values.ndim - 2) + (half_dim,)
    cosine = jnp.cos(angles).reshape(new_shape)
    sine = jnp.sin(angles).reshape(new_shape)
    first_half = values[..., :half_dim]
    second_half = values[..., half_dim:]
    return jnp.concatenate(
        [first_half * cosine - second_half * sine, first_half * sine + second_half * cosine],
        axis=-1,
    )


def swap(value, axis, distance):
    size = lax.axis_size(axis)
    return lax.ppermute(value, axis, [(i, i ^ distance) for i in range(size)])


def take_block(array, index, size, axis=0):
    return lax.dynamic_slice_in_dim(array, index * size, size, axis)


def full_spec():
    return pl.BlockSpec(memory_space=pltpu.VMEM)


def call(kernel, outs, operands, scalars=(), scratch=(), resident=(), hbm=(), anywhere=()):
    hbm = [pltpu.with_memory_space_constraint(array, pltpu.HBM) for array in hbm]
    resident = [pltpu.with_memory_space_constraint(array, pltpu.VMEM) for array in resident]
    hbm += anywhere
    specs = [pl.BlockSpec(memory_space=pl.ANY)] * len(hbm)
    specs += [full_spec()] * (len(operands) + len(resident))
    arrays = [*hbm, *operands, *resident]
    specs = [pl.BlockSpec(memory_space=pltpu.SMEM)] * len(scalars) + specs
    arrays = [*scalars, *arrays]
    return pl.pallas_call(
        kernel,
        out_shape=tuple(outs),
        in_specs=specs,
        out_specs=tuple(full_spec() for _ in outs),
        scratch_shapes=scratch,
        cost_estimate=pl.CostEstimate(flops=1000, bytes_accessed=1000, transcendentals=0),
        compiler_params=pltpu.CompilerParams(vmem_limit_bytes=KERNEL_VMEM),
    )(*arrays)


def shaped(shape, dtype):
    return jax.ShapeDtypeStruct(shape, dtype)


def norm_kernel(
    n_adapter, voices, books, place_ref,
    tokens_hbm, gain_hbm, label_hbm, lengths_hbm, closing_hbm, delays_hbm,
    own_ref, rows_ref, out1_ref, out2_ref, out3_ref, placing_ref, raw_ref, active_ref, closing_ref,
    normed_ref, tokens_ref, gain_ref, label_ref, lengths_ref, delays_ref, sems,
):
    a, t = place_ref[0], place_ref[1]
    streams, model_width = tokens_ref.shape
    d_slice = own_ref.shape[1]
    closing_part = closing_hbm.at[:, pl.ds(pl.multiple_of(a * d_slice, d_slice), d_slice)]
    copies = [
        pltpu.make_async_copy(source, target, sems.at[i])
        for i, (source, target) in enumerate(
            (
                (tokens_hbm, tokens_ref),
                (gain_hbm, gain_ref),
                (label_hbm, label_ref),
                (lengths_hbm, lengths_ref),
                (closing_part, closing_ref),
                (delays_hbm, delays_ref),
            )
        )
    ]
    for copy in copies:
        copy.start()
    for copy in copies:
        copy.wait()
    half = streams // 2
    cap = rows_ref.shape[0]
    tok = tokens_ref[...].astype(jnp.float32)
    mean = jnp.sum(tok * tok, axis=-1, keepdims=True) * (1.0 / model_width)
    normed_ref[...] = (tok * lax.rsqrt(mean + NORM_EPS) * gain_ref[...]).astype(jnp.bfloat16)

    def owner_of(label):
        return sum((label >= j * voices).astype(jnp.int32) for j in range(1, n_adapter))

    square = (streams, streams)
    row_index = lax.broadcasted_iota(jnp.int32, square, 0)
    col_index = lax.broadcasted_iota(jnp.int32, square, 1)

    def column(row):
        picked = jnp.where(row_index == col_index, row.astype(jnp.float32), 0.0)
        return jnp.sum(picked, axis=1, keepdims=True).astype(jnp.int32)

    label_row = label_ref[...]
    label_col = column(label_row)
    owner_row, owner_col = owner_of(label_row), owner_of(label_col)
    voice = label_col - owner_col * voices
    earlier = (owner_col == owner_row) & (row_index < col_index)
    rank = jnp.sum(earlier.astype(jnp.float32), axis=0, keepdims=True).astype(jnp.int32)
    slot = jnp.bitwise_xor(owner_row, a) * cap + rank
    slots = (n_adapter * cap, streams)
    placing = (lax.broadcasted_iota(jnp.int32, slots, 0) == slot).astype(jnp.float32).astype(jnp.bfloat16)
    placing_ref[...] = placing
    lanes = (streams, 128)
    onehot = (lax.broadcasted_iota(jnp.int32, lanes, 1) == voice).astype(jnp.float32).astype(jnp.bfloat16)
    mine = normed_ref[:, pl.ds(pl.multiple_of(t * d_slice, d_slice), d_slice)]
    rows = jnp.dot(placing, mine, preferred_element_type=jnp.float32).astype(jnp.bfloat16)
    kinds = jnp.dot(placing, onehot, preferred_element_type=jnp.float32).astype(jnp.bfloat16)
    own_ref[...] = normed_ref[:, pl.ds(pl.multiple_of(a * d_slice, d_slice), d_slice)]
    rows_ref[:, :d_slice] = rows[:cap]
    rows_ref[:, d_slice:] = kinds[:cap]
    first = pl.multiple_of(lax.rem(t, 2) * half, half)
    length_col = column(lengths_ref[...])
    lane = lax.broadcasted_iota(jnp.int32, active_ref.shape, 1)
    active = jnp.zeros(active_ref.shape, jnp.float32)
    books_row = delays_ref[...].astype(jnp.float32)
    book = lax.broadcasted_iota(jnp.int32, books_row.shape, 1)
    for p in range(books):
        mine_only = jnp.where(book == t * books + p, books_row, 0.0)
        delay = jnp.sum(mine_only, axis=1, keepdims=True).astype(jnp.int32)
        started = (length_col >= delay).astype(jnp.float32)
        active = jnp.where(lane == p, started, active)
    active_ref[...] = active
    quarter = raw_ref.shape[2]
    for k in range(n_adapter):
        first_raw = pl.multiple_of(jnp.bitwise_xor(a, k) * d_slice + t * quarter, quarter)
        raw_ref[k] = tokens_ref[:, pl.ds(first_raw, quarter)]
    for k, out_ref in enumerate((out1_ref, out2_ref, out3_ref), 1):
        start = pl.multiple_of(jnp.bitwise_xor(a, k) * d_slice, d_slice)
        out_ref[:half, :d_slice] = normed_ref[pl.ds(first, half), pl.ds(start, d_slice)]
        out_ref[:half, d_slice:] = jnp.zeros((half, 128), jnp.bfloat16)
        out_ref[half:, :d_slice] = rows[k * cap : (k + 1) * cap]
        out_ref[half:, d_slice:] = kinds[k * cap : (k + 1) * cap]


def fetch_kernel(question_hbm, content_hbm, after_hbm, question_ref, content_ref, sems):
    copies = []
    for source, target in ((question_hbm, question_ref), (content_hbm, content_ref)):
        rows = source.shape[0] // 4
        for i in range(4):
            part = pl.ds(i * rows, rows)
            copies.append(
                pltpu.make_async_copy(source.at[part], target.at[part], sems.at[len(copies)])
            )
    for copy in copies:
        copy.start()
    for copy in copies:
        copy.wait()


def lowering_kernel(
    voices, rank, own_ref, in1_ref, in2_ref, in3_ref, question_ref, content_ref, down_ref, onehot_ref
):
    width = question_ref.shape[1]
    cap = own_ref.shape[0]
    rows = jnp.concatenate(
        [own_ref[...], in1_ref[cap:, :], in2_ref[cap:, :], in3_ref[cap:, :]], axis=0
    )
    onehot = rows[:, width:]
    onehot_ref[...] = onehot
    onehot = onehot.astype(jnp.float32)
    left = lax.broadcasted_iota(jnp.int32, (rows.shape[0], 2 * rank), 1) < rank
    sums = []
    for weight_ref in (question_ref, content_ref):
        every = lax.dot_general(
            rows[:, :width],
            weight_ref[...],
            (((1,), (1,)), ((), ())),
            preferred_element_type=jnp.float32,
        )
        kept = 0.0
        for pair in range(voices // 2):
            mask = jnp.where(left, onehot[:, 2 * pair : 2 * pair + 1], onehot[:, 2 * pair + 1 : 2 * pair + 2])
            kept = kept + mask * every[:, 2 * pair * rank : 2 * (pair + 1) * rank]
        sums.append(kept[:, :rank] + kept[:, rank:])
    down_ref[...] = jnp.concatenate(sums, axis=1)


def raising_kernel(
    voices, rank, near_ref, far_ref, onehot_ref, question_ref, content_ref,
    own_ref, out1_ref, out2_ref, out3_ref,
):
    down = (near_ref[...] + far_ref[...]).astype(jnp.bfloat16).astype(jnp.float32)
    onehot = onehot_ref[...].astype(jnp.float32)
    left = lax.broadcasted_iota(jnp.int32, (down.shape[0], 2 * rank), 1) < rank
    first = 0
    for i, weight_ref in enumerate((question_ref, content_ref)):
        part = down[:, i * rank : (i + 1) * rank]
        twice = jnp.concatenate([part, part], axis=1)
        spread = jnp.concatenate(
            [
                jnp.where(left, onehot[:, 2 * pair : 2 * pair + 1], onehot[:, 2 * pair + 1 : 2 * pair + 2])
                * twice
                for pair in range(voices // 2)
            ],
            axis=1,
        ).astype(jnp.bfloat16)
        up = jnp.dot(spread, weight_ref[...], preferred_element_type=jnp.float32) * ADAPTER_SCALE
        up = up.astype(jnp.bfloat16)
        last = first + weight_ref.shape[1]
        cap = own_ref.shape[0]
        for k, out_ref in enumerate((own_ref, out1_ref, out2_ref, out3_ref)):
            out_ref[:, first:last] = up[k * cap : (k + 1) * cap]
        first = last


def base_kernel(
    place_ref, own_ref, in1_ref, in2_ref, in3_ref, other_ref, query_ref, key_ref, value_ref,
    keep_ref, send_ref, rows_ref,
):
    core = lax.rem(place_ref[1], 2)
    streams, width = own_ref.shape
    half = streams // 2
    rows_ref[:streams, :] = own_ref[...]
    for k, in_ref in enumerate((in1_ref, in2_ref, in3_ref), 1):
        mine = pl.multiple_of(k * streams + core * half, half)
        theirs = pl.multiple_of(k * streams + (1 - core) * half, half)
        rows_ref[pl.ds(mine, half), :] = in_ref[:half, :width]
        rows_ref[pl.ds(theirs, half), :] = other_ref[(k - 1) * half : k * half, :]
    first = 0
    for weight_ref in (query_ref, key_ref, value_ref):
        last = first + weight_ref.shape[1]
        out = jnp.dot(rows_ref[...], weight_ref[...], preferred_element_type=jnp.float32)
        for k in range(4):
            out_ref = send_ref if k % 2 else keep_ref
            out_ref[k // 2 * streams : (k // 2 + 1) * streams, first:last] = out[
                k * streams : (k + 1) * streams
            ]
        first = last


def out_kernel(
    place_ref, own_ref, in1_ref, in2_ref, in3_ref, weight_ref, keep_ref, send_ref, rows_ref
):
    turn = jnp.bitwise_xor(place_ref[0], place_ref[1])
    streams = own_ref.shape[0]
    for k, in_ref in enumerate((own_ref, in1_ref, in2_ref, in3_ref)):
        first = pl.multiple_of(jnp.bitwise_xor(turn, k) * streams, streams)
        rows_ref[pl.ds(first, streams), :] = in_ref[...]
    depth = weight_ref.shape[0]
    quarter = rows_ref.shape[1] - depth
    column = pl.ds(pl.multiple_of(place_ref[1] * quarter, quarter), quarter)
    out = jnp.dot(rows_ref[:, :depth], weight_ref[...], preferred_element_type=jnp.float32)
    for m in range(4):
        out_ref = send_ref if m % 2 else keep_ref
        to, block = pl.ds(m // 2 * streams, streams), slice(m * streams, (m + 1) * streams)
        out_ref[to, :] = out[block]
        out_ref[to, column] += rows_ref[block, depth:].astype(jnp.float32)


def head_kernel(
    first, place_ref, own_ref, across_ref, pair_ref, scale_ref, gain_ref, weight_ref, keep_ref, send_ref, rows_ref
):
    turn = jnp.bitwise_xor(place_ref[0], place_ref[1])
    streams = own_ref.shape[0]
    diagonal = lax.broadcasted_iota(jnp.int32, (streams, streams), 0) == lax.broadcasted_iota(
        jnp.int32, (streams, streams), 1
    )
    pieces = (
        own_ref[...],
        pair_ref[:streams, :],
        across_ref[...],
        pair_ref[streams:, :],
    )
    for m, piece in enumerate(pieces):
        row = (0, 2, 1, 3)[m]
        scale = jnp.sum(
            jnp.where(diagonal, scale_ref[row : row + 1, :], 0.0), axis=1, keepdims=True
        )
        at = pl.multiple_of(jnp.bitwise_xor(turn, m) * streams, streams)
        rows_ref[pl.ds(at, streams), :] = (
            piece.astype(jnp.float32) * scale * gain_ref[...]
        ).astype(jnp.bfloat16)
    columns_kernel(first, rows_ref, weight_ref, keep_ref, send_ref)


def columns_kernel(first, rows_ref, weight_ref, keep_ref, send_ref):
    streams = keep_ref.shape[0] // 2
    width = keep_ref.shape[1]
    out = 16.0 * jnp.dot(
        rows_ref[...], weight_ref[:, first : first + width], preferred_element_type=jnp.float32
    )
    keep_ref[:streams] = out[:streams]
    send_ref[:streams] = out[streams : 2 * streams]
    keep_ref[streams:] = out[2 * streams : 3 * streams]
    send_ref[streams:] = out[3 * streams :]


LEVELS = 30719.0
LEVEL_STEP = 16416.0 / LEVELS


def row_root(values):
    largest = jnp.max(jnp.abs(values), axis=1, keepdims=True)
    root = jnp.sqrt(16384.0 / jnp.maximum(largest, 1e-30))
    return lax.reduce_precision(jnp.minimum(root, 65504.0), 5, 10)


def encode(values, root):
    scaled = values * (root * root) * (1.0 / LEVEL_STEP)
    place = (jnp.round(jnp.abs(scaled)) + 1024.0) * (1.0 / 1024.0)
    power = jnp.floor(place)
    size = (1.0 + (place - power)) * jnp.exp2(power - 15.0)
    code = jnp.where(scaled < 0, -size, size).astype(jnp.float16)
    root = jnp.broadcast_to(root.astype(jnp.float16), (values.shape[0], 128))
    return jnp.concatenate([code, root], axis=1)


def decode(coded, width):
    code = coded[:, :width].astype(jnp.float32)
    root = coded[:, width : width + 1].astype(jnp.float32)
    size = jnp.abs(code)
    power = jnp.floor(jnp.log2(size))
    steps = jnp.round((power + 14.0 + (size * jnp.exp2(-power) - 1.0)) * 1024.0)
    return jnp.where(code < 0, -steps, steps) * (LEVEL_STEP / (root * root))


def per_device_four(
    tokens,
    attention_gain,
    query_weight,
    key_weight,
    value_weight,
    speaker_question_lowering,
    speaker_question_raising,
    speaker_content_lowering,
    speaker_content_raising,
    rotated_key_cache,
    stored_value_cache,
    sequence_speaker_label,
    lengths,
    output_weight,
    closing_gain,
    codebook_weight,
    delays,
):
    n_adapter = lax.axis_size("adapter")
    peers = range(1, n_adapter)
    a = lax.axis_index("adapter")
    t = lax.axis_index("tensor")
    str_dev, model_width = tokens.shape
    place_ids = jnp.stack([a, t]).astype(jnp.int32)
    d_slice = model_width // n_adapter
    voices, rank = speaker_question_raising.shape[:2]
    query_columns = query_weight.shape[1]
    key_value_columns = key_weight.shape[1]

    bf16 = jnp.bfloat16
    slot_cap = max(2, 2 * str_dev // n_adapter)
    half = str_dev // 2
    n_tensor = lax.axis_size("tensor")
    quarter = d_slice // n_tensor
    books_local = CB // n_tensor
    own_cols, own_rows, *outgoing, placing, raw, active, final_slice = call(
        functools.partial(norm_kernel, n_adapter, voices, books_local),
        [shaped((str_dev, d_slice), bf16), shaped((slot_cap, d_slice + 128), bf16)]
        + [shaped((half + slot_cap, d_slice + 128), bf16)] * 3
        + [
            shaped((n_adapter * slot_cap, str_dev), bf16),
            shaped((n_adapter, str_dev, quarter), bf16),
            shaped((str_dev, 128), jnp.float32),
            shaped((1, d_slice), jnp.float32),
        ],
        [],
        [place_ids],
        [
            pltpu.VMEM((str_dev, model_width), bf16),
            pltpu.VMEM((str_dev, model_width), bf16),
            pltpu.VMEM((1, model_width), jnp.float32),
            pltpu.VMEM((1, str_dev), jnp.int32),
            pltpu.VMEM((1, str_dev), jnp.int32),
            pltpu.VMEM((1, CB), jnp.int32),
            pltpu.SemaphoreType.DMA((6,)),
        ],
        hbm=[
            tokens,
            attention_gain[None],
            sequence_speaker_label[None],
            lengths[None],
            closing_gain[None],
            delays[None],
        ],
    )
    came = [swap(payload, "adapter", k) for k, payload in zip(peers, outgoing)]
    question_down, content_down = call(
        fetch_kernel,
        [pltpu.VMEM((voices * rank, d_slice), bf16)] * 2,
        [],
        scratch=[pltpu.SemaphoreType.DMA((8,))],
        hbm=[
            speaker_question_lowering.transpose(1, 2, 0).reshape(voices * rank, d_slice),
            speaker_content_lowering.transpose(1, 2, 0).reshape(voices * rank, d_slice),
        ],
        anywhere=[own_cols],
    )
    came, question_down = lax.optimization_barrier((came, question_down))
    other = swap(jnp.concatenate([piece[:half, :d_slice] for piece in came]), "tensor", 1)

    down, onehot = call(
        functools.partial(lowering_kernel, voices, rank),
        [shaped((n_adapter * slot_cap, 2 * rank), jnp.float32), shaped((n_adapter * slot_cap, 128), bf16)],
        [own_rows, *came],
        resident=[question_down, content_down],
    )
    other, down = lax.optimization_barrier((other, down))
    kept, sent = call(
        base_kernel,
        [shaped((2 * str_dev, query_columns + 2 * key_value_columns), jnp.float32)] * 2,
        [own_cols, *came, other],
        [place_ids],
        [pltpu.VMEM((n_adapter * str_dev, d_slice), bf16)],
        resident=[query_weight, key_weight, value_weight],
    )
    down = down + swap(down, "tensor", 1)
    summed = kept + swap(sent, "adapter", 1)
    raised = call(
        functools.partial(raising_kernel, voices, rank),
        [shaped((slot_cap, query_columns + key_value_columns), bf16)] * n_adapter,
        [down, swap(down, "tensor", 2), onehot],
        resident=[
            speaker_question_raising.reshape(voices * rank, query_columns),
            speaker_content_raising.reshape(voices * rank, key_value_columns),
        ],
    )
    returned = jnp.concatenate(
        [raised[0]] + [swap(raised[k], "adapter", k) for k in peers], axis=0
    )
    adapter_summands = jnp.einsum(
        "ms,mc->sc", placing, returned, preferred_element_type=jnp.float32
    )

    far = swap(summed[str_dev:], "adapter", 2)
    projected = summed[:str_dev] + far
    kv_local, ctx_len, head_dim = rotated_key_cache.shape[1:]
    group_size = query_columns // (kv_local * head_dim)
    query = rotate(
        (projected[:, :query_columns] + adapter_summands[:, :query_columns]).reshape(
            str_dev, kv_local, group_size, head_dim
        ),
        lengths,
    ).astype(jnp.bfloat16)
    key_base = projected[:, query_columns : query_columns + key_value_columns]
    key_new = rotate(key_base.reshape(str_dev, kv_local, head_dim), lengths).astype(jnp.bfloat16)
    value_new = (
        (projected[:, query_columns + key_value_columns :] + adapter_summands[:, query_columns:])
        .reshape(str_dev, kv_local, head_dim)
        .astype(jnp.bfloat16)
    )
    scale_factor = 1.0 / head_dim**0.5
    scores = (
        jnp.einsum("skgd,skcd->skgc", query, rotated_key_cache, preferred_element_type=jnp.float32)
        * scale_factor
    )
    own_score = (
        jnp.einsum("skgd,skd->skg", query, key_new, preferred_element_type=jnp.float32)
        * scale_factor
    )
    valid = (jnp.arange(ctx_len)[None, :] < lengths[:, None])[:, None, None, :]
    masked = jnp.where(valid, scores, -1e30)
    top_score = jnp.maximum(jnp.max(masked, axis=-1), own_score)
    weights_all = jnp.where(valid, jnp.exp(scores - top_score[..., None]), 0.0)
    own_weight = jnp.exp(own_score - top_score)
    total = jnp.sum(weights_all, axis=-1) + own_weight
    probs = (weights_all / total[..., None]).astype(jnp.bfloat16)
    own_prob = (own_weight / total).astype(jnp.bfloat16)
    mixed = jnp.einsum(
        "skgc,skcd->skgd", probs, stored_value_cache, preferred_element_type=jnp.float32
    )
    mixed = (
        mixed
        + own_prob.astype(jnp.float32)[..., None] * value_new.astype(jnp.float32)[:, :, None, :]
    )
    attended = mixed.astype(jnp.bfloat16).reshape(str_dev, query_columns)

    def with_raw(k):
        return jnp.concatenate([attended, raw[k]], axis=1)

    kept, sent = call(
        out_kernel,
        [shaped((2 * str_dev, d_slice), jnp.float32)] * 2,
        [with_raw(0)] + [swap(with_raw(k), "adapter", k) for k in peers],
        [place_ids],
        [pltpu.VMEM((n_adapter * str_dev, query_columns + quarter), bf16)],
        resident=[output_weight],
    )
    pair = kept + swap(sent, "tensor", 1)
    pair_scale = row_root(pair[str_dev:])
    coded = swap(encode(pair[str_dev:], pair_scale), "tensor", 2)
    arrived = decode(coded, d_slice)
    summed_out = pair[:str_dev] + arrived
    hidden_out = summed_out.astype(jnp.bfloat16)

    hidden_f = hidden_out.astype(jnp.float32)
    square = jnp.sum(hidden_f * hidden_f, axis=-1)
    square_sum = square
    for k in peers:
        square_sum = square_sum + swap(square, "adapter", k)
    scale = lax.rsqrt(square_sum / model_width + NORM_EPS)[None]
    across = swap(hidden_out, "tensor", 2)
    hidden_pair = swap(jnp.concatenate([hidden_out, across]), "tensor", 1)
    scale = jnp.concatenate([scale, swap(scale, "tensor", 2)])
    scale = jnp.concatenate([scale, swap(scale, "tensor", 1)])

    width = codebook_weight.shape[1] // 2
    outs = []

    def moved(block, k):
        return swap(block.astype(jnp.float16), "adapter", k).astype(jnp.float32)

    sums = [shaped((2 * str_dev, width), jnp.float32)] * 2
    kept, sent, final_rows = call(
        functools.partial(head_kernel, 0),
        sums + [shaped((n_adapter * str_dev, d_slice), bf16)],
        [hidden_out, across, hidden_pair, scale, final_slice],
        [place_ids],
        resident=[codebook_weight],
    )
    kept_far, sent_far = call(
        functools.partial(columns_kernel, width), sums, [final_rows], resident=[codebook_weight]
    )
    kept = kept + moved(sent, 1)
    first_total = kept[:str_dev] + moved(kept[str_dev:], 2)
    second_total = (
        kept_far[:str_dev]
        + moved(sent_far[:str_dev], 1)
        + moved(kept_far[str_dev:], 2)
        + moved(sent_far[str_dev:], 3)
    )
    outs = [first_total * (1.0 / 16.0), second_total * (1.0 / 16.0)]
    if width == VOC:
        logits = jnp.stack([out * active[:, p : p + 1] for p, out in enumerate(outs)], axis=1)
    else:
        logits = jnp.concatenate(outs, axis=1).reshape(str_dev, books_local, VOC)
        logits = logits * active[:, :books_local, None]
    return (hidden_out, logits)


def per_device(
    tokens,
    attention_gain,
    query_weight,
    key_weight,
    value_weight,
    speaker_question_lowering,
    speaker_question_raising,
    speaker_content_lowering,
    speaker_content_raising,
    rotated_key_cache,
    stored_value_cache,
    sequence_speaker_label,
    lengths,
    output_weight,
    closing_gain,
    codebook_weight,
    delays,
):
    n_adapter = lax.axis_size("adapter")
    n_tensor = lax.axis_size("tensor")
    adapter_pos = lax.axis_index("adapter")
    tensor_pos = lax.axis_index("tensor")
    str_dev, model_width = tokens.shape
    all_streams = str_dev * n_adapter
    d_slice = model_width // n_adapter
    tensor_width = model_width // n_tensor
    tok_f = tokens.astype(jnp.float32)
    inverse = lax.rsqrt(jnp.mean(tok_f * tok_f, axis=-1, keepdims=True) + NORM_EPS)
    rescaled_hidden_state = (tok_f * inverse * attention_gain).astype(jnp.bfloat16)
    raw_cols, norm_cols = (
        lax.all_to_all(tokens, "adapter", split_axis=1, concat_axis=0, tiled=True),
        lax.all_to_all(rescaled_hidden_state, "adapter", split_axis=1, concat_axis=0, tiled=True),
    )
    query_columns = query_weight.shape[1]
    key_value_columns = key_weight.shape[1]
    weights_cat = jnp.concatenate([query_weight, key_weight, value_weight], axis=1)
    full_proj = jnp.dot(norm_cols, weights_cat, preferred_element_type=jnp.float32)
    summed = lax.psum(full_proj, "adapter")
    projected = lax.dynamic_slice_in_dim(summed, adapter_pos * str_dev, str_dev, 0)
    plain_query = projected[:, :query_columns]
    key_base = projected[:, query_columns : query_columns + key_value_columns]
    plain_value = projected[:, query_columns + key_value_columns :]
    voices_per_shard = speaker_question_raising.shape[0]
    adapter_rank_size = speaker_question_raising.shape[1]
    slot_cap = max(2, 2 * str_dev // n_adapter)
    slot_total = n_adapter * slot_cap
    owner_ids = sequence_speaker_label // voices_per_shard
    local_voice = sequence_speaker_label % voices_per_shard
    same_owner = owner_ids[:, None] == owner_ids[None, :]
    earlier = jnp.arange(str_dev)[:, None] > jnp.arange(str_dev)[None, :]
    owner_rank = jnp.sum((same_owner & earlier).astype(jnp.int32), axis=1)
    slot_ids = owner_ids * slot_cap + owner_rank
    placing = (slot_ids[None, :] == jnp.arange(slot_total)[:, None]).astype(jnp.bfloat16)
    voice_onehot = (local_voice[:, None] == jnp.arange(voices_per_shard)[None, :]).astype(
        jnp.bfloat16
    )
    normed_part = lax.dynamic_slice_in_dim(
        rescaled_hidden_state, tensor_pos * tensor_width, tensor_width, 1
    )
    send_rows = jnp.dot(placing, normed_part, preferred_element_type=jnp.float32).astype(
        jnp.bfloat16
    )
    send_voice = jnp.dot(placing, voice_onehot, preferred_element_type=jnp.float32).astype(
        jnp.bfloat16
    )
    send_rows = send_rows.reshape(n_adapter, slot_cap, tensor_width)
    send_voice = send_voice.reshape(n_adapter, slot_cap, voices_per_shard)
    query_down_matrix = speaker_question_lowering.reshape(
        tensor_width, voices_per_shard * adapter_rank_size
    )
    value_down_matrix = speaker_content_lowering.reshape(
        tensor_width, voices_per_shard * adapter_rank_size
    )
    query_up_matrix = speaker_question_raising.reshape(
        voices_per_shard * adapter_rank_size, query_columns
    )
    value_up_matrix = speaker_content_raising.reshape(
        voices_per_shard * adapter_rank_size, key_value_columns
    )
    rows_in = lax.all_to_all(send_rows, "adapter", split_axis=0, concat_axis=0, tiled=True)
    voices_in = lax.all_to_all(send_voice, "adapter", split_axis=0, concat_axis=0, tiled=True)
    item_count = rows_in.shape[1]
    flat_rows = rows_in.reshape(-1, tensor_width)
    onehot_b = voices_in.reshape(-1, voices_per_shard)
    onehot_f = onehot_b.astype(jnp.float32)
    all_q = jnp.dot(flat_rows, query_down_matrix, preferred_element_type=jnp.float32).reshape(
        -1, voices_per_shard, adapter_rank_size
    )
    all_v = jnp.dot(flat_rows, value_down_matrix, preferred_element_type=jnp.float32).reshape(
        -1, voices_per_shard, adapter_rank_size
    )
    down_q = jnp.sum(onehot_f[:, :, None] * all_q, axis=1)
    down_v = jnp.sum(onehot_f[:, :, None] * all_v, axis=1)
    down_q, down_v = lax.psum((down_q, down_v), "tensor")
    query_broadcast = (onehot_b[:, :, None] * down_q.astype(jnp.bfloat16)[:, None, :]).reshape(
        -1, voices_per_shard * adapter_rank_size
    )
    value_broadcast = (onehot_b[:, :, None] * down_v.astype(jnp.bfloat16)[:, None, :]).reshape(
        -1, voices_per_shard * adapter_rank_size
    )
    question_raised_product = (
        jnp.dot(query_broadcast, query_up_matrix, preferred_element_type=jnp.float32)
        * ADAPTER_SCALE
    ).astype(jnp.bfloat16)
    content_raised_product = (
        jnp.dot(value_broadcast, value_up_matrix, preferred_element_type=jnp.float32)
        * ADAPTER_SCALE
    ).astype(jnp.bfloat16)
    outgoing = jnp.concatenate([question_raised_product, content_raised_product], axis=1).reshape(
        n_adapter, item_count, query_columns + key_value_columns
    )
    returned = lax.all_to_all(outgoing, "adapter", split_axis=0, concat_axis=0, tiled=True)
    adapter_summands = jnp.einsum(
        "ms,mc->sc",
        placing,
        returned.reshape(slot_total, query_columns + key_value_columns),
        preferred_element_type=jnp.float32,
    )
    kv_local = rotated_key_cache.shape[1]
    head_dim = rotated_key_cache.shape[3]
    ctx_len = rotated_key_cache.shape[2]
    group_size = query_columns // (kv_local * head_dim)
    adapted_query = (plain_query + adapter_summands[:, :query_columns]).reshape(
        str_dev, kv_local, group_size, head_dim
    )
    query = rotate(adapted_query, lengths).astype(jnp.bfloat16)
    key_new = rotate(key_base.reshape(str_dev, kv_local, head_dim), lengths).astype(jnp.bfloat16)
    value_new = (
        (plain_value + adapter_summands[:, query_columns:])
        .reshape(str_dev, kv_local, head_dim)
        .astype(jnp.bfloat16)
    )
    scale_factor = 1.0 / head_dim**0.5
    scores = (
        jnp.einsum("skgd,skcd->skgc", query, rotated_key_cache, preferred_element_type=jnp.float32)
        * scale_factor
    )
    own_score = (
        jnp.einsum("skgd,skd->skg", query, key_new, preferred_element_type=jnp.float32)
        * scale_factor
    )
    valid = (jnp.arange(ctx_len)[None, :] < lengths[:, None])[:, None, None, :]
    masked = jnp.where(valid, scores, -1e30)
    top_score = jnp.maximum(jnp.max(masked, axis=-1), own_score)
    weights_all = jnp.where(valid, jnp.exp(scores - top_score[..., None]), 0.0)
    own_weight = jnp.exp(own_score - top_score)
    total = jnp.sum(weights_all, axis=-1) + own_weight
    probs = (weights_all / total[..., None]).astype(jnp.bfloat16)
    own_prob = (own_weight / total).astype(jnp.bfloat16)
    mixed = jnp.einsum(
        "skgc,skcd->skgd", probs, stored_value_cache, preferred_element_type=jnp.float32
    )
    mixed = (
        mixed
        + own_prob.astype(jnp.float32)[..., None] * value_new.astype(jnp.float32)[:, :, None, :]
    )
    attended = mixed.astype(jnp.bfloat16).reshape(str_dev, query_columns)
    partial_out = jnp.dot(
        lax.all_gather(attended, "adapter", axis=0, tiled=True),
        output_weight,
        preferred_element_type=jnp.float32,
    )
    final_slice = lax.dynamic_slice_in_dim(closing_gain, adapter_pos * d_slice, d_slice)
    rows_tensor = all_streams // n_tensor
    summed_out = lax.psum(partial_out, "tensor")
    hidden_all = (raw_cols.astype(jnp.float32) + summed_out).astype(jnp.bfloat16)
    hidden_f = hidden_all.astype(jnp.float32)
    square_sum = lax.psum(jnp.sum(hidden_f * hidden_f, axis=-1), "adapter")
    final_normed = (
        hidden_f * lax.rsqrt(square_sum / model_width + NORM_EPS)[:, None] * final_slice
    ).astype(jnp.bfloat16)
    hidden_out = lax.dynamic_slice_in_dim(hidden_all, tensor_pos * rows_tensor, rows_tensor, 0)
    logit_rows = lax.psum_scatter(
        jnp.dot(final_normed, codebook_weight, preferred_element_type=jnp.float32),
        "adapter",
        scatter_dimension=0,
        tiled=True,
    )
    books_local = CB // n_tensor
    book_delays = lax.dynamic_slice_in_dim(delays, tensor_pos * books_local, books_local)
    active = (lengths[:, None] >= book_delays[None, :]).astype(jnp.float32)
    logits = logit_rows.reshape(str_dev, books_local, VOC) * active[:, :, None]
    return (hidden_out, logits)


def solution(mesh):
    in_specs = (
        P(("groups", "adapter"), None),
        P(),
        P("adapter", "tensor"),
        P("adapter", "tensor"),
        P("adapter", "tensor"),
        P("tensor", "adapter", None),
        P("adapter", None, "tensor"),
        P("tensor", "adapter", None),
        P("adapter", None, "tensor"),
        P(("groups", "adapter"), "tensor", None, None),
        P(("groups", "adapter"), "tensor", None, None),
        P(("groups", "adapter")),
        P(("groups", "adapter")),
        P("tensor", "adapter"),
        P(),
        P("adapter", "tensor"),
        P(),
    )
    out_specs = (P(("groups", "tensor"), "adapter"), P(("groups", "adapter"), "tensor", None))
    four = mesh.shape["adapter"] == 4 and mesh.shape["tensor"] == 4
    return jax.shard_map(
        per_device_four if four else per_device, mesh=mesh, in_specs=in_specs, out_specs=out_specs, check_vma=False
    )
```
